32 devices in a mesh: slide: 4 (over y, x), seq: 8 (over z, core).
Axes of the slice: x: 2, y: 2, z: 4, core: 2. Of those that a mesh axis runs over, the one named last changes fastest.
Arguments:
- query_tiles: bfloat16 [32768, 768], P(('slide', 'seq')), parts along dimension 0, may hold values from -160 to 160
- key_tiles: bfloat16 [32768, 768], P(('slide', 'seq')), parts along dimension 0, may hold values from -4.04 to 4.04
- value_tiles: bfloat16 [32768, 768], P(('slide', 'seq')), parts along dimension 0, may hold values from -6 to 6
- slide_length: int32 [4], P('slide'), parts along dimension 0, may hold values from 7680 to 8192
Outputs:
- attended: bfloat16 [32768, 768], P(('slide', 'seq')), parts along dimension 0
The draws below stay inside these ranges and needn't reach their ends.
There are 4 independent parts, one for each index of `slide`. The reference program is written for one: setup_inputs(seed, part) draws one part's arguments, and reference() takes and returns one part's arrays. A program takes and returns all parts, laid end to end along the dimension named above; each array names one. Nothing has to cross between parts.
All inputs are finite; a program needn't handle non-finite values.
Results may differ from the reference program's by a relative error of at most 0.0045.
Values may be sent and summed in bfloat16 or wider, within the bound.
A program may use at most 128 MiB of HBM per device.

```python
from functools import reduce
import jax
import jax.numpy as jnp
import numpy as np
from jax import lax

HEADS = 12
HEAD_DIM = 64
WIDTH = 768
TOK_DEV = 1024
TOKENS = 8192
SEG0 = 512
BRANCHES = 5


def shared_rows(key):
    base = jnp.clip(jax.random.normal(jax.random.fold_in(key, 11), (TOKENS, WIDTH), jnp.float32), -4.0, 4.0)
    return base


def draw_key_tiles(key, part):
    base = shared_rows(key)
    return base.astype(jnp.bfloat16)


def draw_query_tiles(key, part):
    key = jax.random.fold_in(key, 2)
    own = jnp.clip(jax.random.normal(key, (TOKENS, WIDTH), jnp.float32), -4.0, 4.0)
    return own.astype(jnp.bfloat16)


def level_of(rng, shape, shards, least, high):
    level, own = 1.0, jax.random.fold_in(rng, 6)
    for axis_at, blocks in shards:
        steps = jnp.exp(jax.random.uniform(jax.random.fold_in(own, axis_at), (blocks,), jnp.float32, least / len(shards), high / len(shards)))
        level = level * jnp.repeat(steps, shape[axis_at] // blocks).reshape([-1 if axis == axis_at else 1 for axis in range(len(shape))])
    return level


def noise(stream_key, shape, width, reach, cuts=(), held_as=jnp.bfloat16):
    values = jax.random.normal(stream_key, shape, jnp.float32) * width
    if len(cuts) > 0:
        values = level_of(stream_key, shape, cuts, -0.22, 0.18) * values
    return jnp.clip(values, min=-reach, max=reach).astype(held_as)


def setup_inputs(seed: int = 0, part: int = 0) -> dict:
    key_of = jax.random.split(jax.random.key(seed), 5)
    part_keys = jax.random.split(jax.random.fold_in(key_of[4], part), 5)
    query_tiles = draw_query_tiles(jax.random.fold_in(jax.random.fold_in(key_of[4], part), 71), part)
    key_tiles = draw_key_tiles(jax.random.fold_in(jax.random.fold_in(key_of[4], part), 71), part)
    value_tiles = noise(part_keys[2], (TOKENS, WIDTH), 1.0, 6.0, ((0, 8),))
    slide_length = jax.random.randint(part_keys[3], (1,), TOKENS - TOK_DEV // 2, TOKENS + 1).astype(jnp.int32)
    return dict(query_tiles=query_tiles, key_tiles=key_tiles, value_tiles=value_tiles, slide_length=slide_length)


scale_factor = 0.125
mask_fill = -1e9
lse_fill = -1e30
ref_block = 1024


def offsets(stride):
    return np.arange(HEADS) % stride


def dilate(source, stride):
    count = source.shape[0] // stride
    shaped = source.reshape(count, stride, HEADS, HEAD_DIM)
    picked = shaped[:, offsets(stride), np.arange(HEADS), :]
    return picked.reshape(count, HEADS * HEAD_DIM)


def spread(compact, stride, fill_value):
    selector = np.arange(stride)[:, None] == offsets(stride)[None, :]
    widened = jnp.where(selector[None, :, :, None], compact[:, None], fill_value)
    return widened.reshape(compact.shape[0] * stride, HEADS, compact.shape[-1])


def attend(query_part, key_part, value_part, key_valid):
    query_count = query_part.shape[0]
    key_count = key_part.shape[0]
    query_heads = query_part.astype(jnp.float32).reshape(query_count, HEADS, HEAD_DIM)
    key_heads = key_part.astype(jnp.float32).reshape(key_count, HEADS, HEAD_DIM)
    value_heads = value_part.astype(jnp.float32).reshape(key_count, HEADS, HEAD_DIM)
    scores = jnp.einsum("qhd,khd->hqk", query_heads, key_heads) * scale_factor
    scores = jnp.where(jnp.transpose(key_valid)[:, None, :], scores, mask_fill)
    row_max = jnp.max(scores, axis=-1, keepdims=True)
    weights = jnp.exp(scores - row_max)
    totals = jnp.sum(weights, axis=-1)
    rounded = lax.optimization_barrier(weights.astype(jnp.bfloat16)).astype(jnp.float32)
    mixed_out = jnp.einsum("hqk,khd->qhd", rounded, value_heads) / jnp.transpose(totals)[:, :, None]
    log_total = jnp.transpose(row_max[..., 0] + jnp.log(totals))
    return mixed_out, log_total


def attend_blocked(query_part, key_part, value_part, key_valid):
    query_count = query_part.shape[0]
    if query_count <= ref_block or query_count % ref_block != 0:
        return attend(query_part, key_part, value_part, key_valid)
    grouped = query_part.reshape(query_count // ref_block, ref_block, query_part.shape[1])

    def one_block(block_queries):
        return attend(block_queries, key_part, value_part, key_valid)

    mixed_out, log_total = lax.map(one_block, grouped)
    return mixed_out.reshape(query_count, HEADS, HEAD_DIM), log_total.reshape(query_count, HEADS)


def reference(query_tiles, key_tiles, value_tiles, slide_length):
    len_bound = slide_length[0]
    parts_out = []
    parts_lse = []
    for branch in range(BRANCHES):
        stride = 2 ** branch
        segment = min(SEG0 * stride, TOKENS) if branch < BRANCHES - 1 else TOKENS
        per_segment = segment // stride
        seg_count = TOKENS // segment
        shaped = [dilate(source, stride).reshape(seg_count, per_segment, HEADS * HEAD_DIM) for source in (query_tiles, key_tiles, value_tiles)]
        positions = (np.arange(TOKENS // stride)[:, None] * stride + offsets(stride)[None, :]).astype(np.int32)
        valid = (jnp.asarray(positions) < len_bound).reshape(seg_count, per_segment, HEADS)

        def one_segment(members):
            return attend_blocked(members[0], members[1], members[2], members[3])

        mixed_out, log_total = lax.map(one_segment, (shaped[0], shaped[1], shaped[2], valid))
        parts_out.append(spread(mixed_out.reshape(TOKENS // stride, HEADS, HEAD_DIM), stride, 0.0))
        parts_lse.append(spread(log_total.reshape(TOKENS // stride, HEADS, 1), stride, lse_fill))
    lse_peak = reduce(jnp.maximum, parts_lse)
    numerator = jnp.zeros((TOKENS, HEADS, HEAD_DIM), jnp.float32)
    denominator = jnp.zeros((TOKENS, HEADS, 1), jnp.float32)
    for branch in range(BRANCHES):
        factor = jnp.exp(parts_lse[branch] - lse_peak)
        numerator = numerator + factor * parts_out[branch]
        denominator = denominator + factor
    blended = (numerator / denominator).reshape(TOKENS, HEADS * HEAD_DIM)
    row_valid = jnp.arange(TOKENS, dtype=jnp.int32) < len_bound
    return jnp.where(row_valid[:, None], blended, 0.0).astype(jnp.bfloat16)
```

```python
import functools
import math

import jax
import jax.numpy as jnp
from jax import lax
from jax.experimental import pallas as pl
from jax.experimental.pallas import tpu as pltpu
from jax.sharding import PartitionSpec as P

HEADS = 12
WIDTH = 768
SEG0 = 512
CLASSES = 16
PAIRS = HEADS // 2
RUN = SEG0 // CLASSES
LANES = 128
MESH = pl.DeviceIdType.MESH
BF16 = jnp.bfloat16
F32 = jnp.float32
EXP_SCALE = 0.125 * math.log2(math.e)
MASK = -1e9


def bitrev(c):
    return (c % 2) * 8 + (c // 2 % 2) * 4 + (c // 4 % 2) * 2 + c // 8 % 2


def rows_at(start, size):
    return pl.ds(pl.multiple_of(start, RUN), size)


def pair_lanes(j, base=0):
    return pl.ds(pl.multiple_of(base + j * LANES, LANES), LANES)


def iota(shape, dim):
    return lax.broadcasted_iota(jnp.int32, shape, dim)


def attend(q, k, v):
    scores = lax.dot_general(q, k, (((1,), (1,)), ((), ())), preferred_element_type=F32)
    peak = jnp.max(scores, axis=1, keepdims=True)
    weights = jnp.exp2((scores - peak) * EXP_SCALE).astype(BF16)
    return jnp.dot(weights, v, preferred_element_type=F32), peak


def merge(acc, peak, acc_b, peak_b):
    top = jnp.maximum(peak, peak_b)
    keep = jnp.exp2((peak - top) * EXP_SCALE)
    add = jnp.exp2((peak_b - top) * EXP_SCALE)
    return acc * keep + acc_b * add, top


def kernel(
    n, len_ref, q_ref, k_ref, v_ref, out_ref,
    qp, kp, vp, r16, r8, r4, bias0, acc_s, peak_s, outp,
    send16, recv16, send8, recv8, send4, recv4, fwd16, fwd8,
):
    shard = q_ref.shape[0]
    segs = shard // SEG0
    chips = n // 2
    me = lax.axis_index("seq")
    chip, core = me // 2, me % 2
    sibling = chip * 2 + 1 - core
    mate_chip = chip + 1 - 2 * (chip % 2)
    mate = mate_chip * 2 + core
    length = len_ref[0]

    barrier = pltpu.get_barrier_semaphore()
    peers = [sibling] + [(chip + step) % chips * 2 + core for step in range(1, chips)]
    for peer in peers:
        pl.semaphore_signal(barrier, inc=1, device_id={"seq": peer}, device_id_type=MESH)

    half = SEG0 // 2
    sub = half // CLASSES
    new = iota((half, half), 0)
    old = iota((half, half), 1)
    shuffle = jnp.where(old == (new % sub) * CLASSES + bitrev(new // sub), 1.0, 0.0).astype(BF16)

    def permute(src, dst):
        def column(step, _):
            lanes = pl.ds(pl.multiple_of(step * 256, 256), 256)
            for t in range(segs):
                for u in range(2):
                    rows = src[pl.ds(t * SEG0 + u * half, half), lanes]
                    moved = jnp.dot(shuffle, rows, preferred_element_type=F32).astype(BF16)
                    for i in range(CLASSES):
                        dst[t, pl.ds(i * RUN + u * sub, sub), lanes] = moved[i * sub:(i + 1) * sub]
            return 0
        lax.fori_loop(0, WIDTH // 256, column, 0)

    permute(k_ref, kp)
    permute(v_ref, vp)

    lane = iota((1, LANES), 1)
    even = jnp.where(lane < 64, 1.0, 0.0).astype(BF16)
    odd = jnp.where(lane < 64, 0.0, 1.0).astype(BF16)
    sides = ((even, odd), (odd, even))

    def gather(j, _):
        for src, base in ((kp, 0), (vp, WIDTH)):
            here = pair_lanes(j)
            there = pair_lanes(j, base)
            for t in range(segs):
                def mixed(shift, keep, size):
                    e = src[t, rows_at(bitrev((2 * j + shift) % keep) * RUN, size), here]
                    o = src[t, rows_at(bitrev((2 * j + 1 + shift) % keep) * RUN, size), here]
                    return e * even + o * odd
                r16[me, pl.ds(t * RUN, RUN), there] = mixed(0, 16, RUN)
                r8[me % 4, pl.ds(t * RUN, RUN), there] = mixed(8, 16, RUN)
                r4[me % 2, pl.ds(t * 2 * RUN, 2 * RUN), there] = mixed(4, 8, 2 * RUN)
        return 0

    lax.fori_loop(0, PAIRS, gather, 0)

    pl.semaphore_wait(barrier, chips)

    def copy(buf, slot, send, recv, peer):
        return pltpu.make_async_remote_copy(
            src_ref=buf.at[slot], dst_ref=buf.at[slot], send_sem=send, recv_sem=recv.at[slot],
            device_id={"seq": peer}, device_id_type=MESH,
        )

    first = []
    for step in range(chips - 1, 0, -1):
        first.append(copy(r16, me, send16.at[step], recv16, (chip + step) % chips * 2 + core))
    first.append(copy(r8, me % 4, send8.at[1], recv8, mate))
    first.append(copy(r16, me, send16.at[0], recv16, sibling))
    first.append(copy(r8, me % 4, send8.at[0], recv8, sibling))
    first.append(copy(r4, me % 2, send4.at[0], recv4, sibling))
    for c in first:
        c.start()

    permute(q_ref, qp)

    row = iota((SEG0, LANES), 0)
    for t in range(segs):
        place = me * shard + t * SEG0 + (row % RUN) * CLASSES + bitrev(row // RUN)
        bias0[t] = jnp.where(place < length, 0.0, MASK).astype(BF16)

    def near(j, _):
        here = pair_lanes(j)
        for side in range(2):
            mine, other = sides[side]
            h = 2 * j + side

            def prep(t, rows):
                k = kp[t, rows, here] * mine + bias0[t, rows, :] * other
                v = vp[t, rows, here] * mine + other
                return k, v

            def query(t, rows):
                return qp[t, rows, here] * mine + other

            for t in range(segs):
                k, v = prep(t, pl.ds(0, SEG0))
                for u in range(2):
                    rows = pl.ds(u * half, half)
                    acc, peak = attend(query(t, rows), k, v)
                    acc_s[h, t, rows, :] = acc
                    peak_s[h, t, rows, :] = jnp.broadcast_to(peak, (half, LANES))
            mid = rows_at((h % 2) * half, half)
            parts = [prep(t, mid) for t in range(segs)]
            k = jnp.concatenate([p[0] for p in parts], axis=0)
            v = jnp.concatenate([p[1] for p in parts], axis=0)
            for t in range(segs):
                acc, peak = attend(query(t, mid), k, v)
                acc, peak = merge(acc_s[h, t, mid, :], peak_s[h, t, mid, :], acc, peak)
                acc_s[h, t, mid, :] = acc
                peak_s[h, t, mid, :] = peak
        return 0

    split = 4
    lax.fori_loop(0, split, near, 0)

    second = []
    for step in range(1, chips):
        source = (chip + chips - step) % chips * 2 + core
        copy(r16, source, send16.at[step], recv16, sibling).wait_recv()
        c = copy(r16, source, fwd16.at[step], recv16, sibling)
        c.start()
        second.append(c)
    copy(r8, mate % 4, send8.at[1], recv8, sibling).wait_recv()
    c = copy(r8, mate % 4, fwd8.at[0], recv8, sibling)
    c.start()
    second.append(c)

    lax.fori_loop(split, PAIRS, near, 0)

    copy(r16, sibling, send16.at[0], recv16, sibling).wait_recv()
    copy(r8, sibling % 4, send8.at[0], recv8, sibling).wait_recv()
    copy(r4, sibling % 2, send4.at[0], recv4, sibling).wait_recv()
    for step in range(1, chips):
        source = (chip + chips - step) % chips * 2 + 1 - core
        copy(r16, source, fwd16.at[step], recv16, sibling).wait_recv()
    far_mate = mate_chip * 2 + 1 - core
    copy(r8, far_mate % 4, fwd8.at[0], recv8, sibling).wait_recv()

    head_lane = 1 - iota((1, LANES), 1) // 64

    def far(j, _):
        here = pair_lanes(j)
        there = pair_lanes(j, WIDTH)
        heads = 2 * j + head_lane

        def bias(slot, size, shift, keep):
            r = iota((size, LANES), 0)
            width = size // segs
            inner = r % width
            place = (
                slot * shard + r // width * SEG0 + inner % RUN * CLASSES
                + inner // RUN * 8 + (heads + shift) % keep
            )
            return jnp.where(place < length, 0.0, MASK).astype(BF16)

        def keys(buf, start, count, size, shift, keep, owner):
            k = buf[pl.ds(start, count), :, here]
            v = buf[pl.ds(start, count), :, there]
            return k, v, bias(owner, size, shift, keep)

        def listed(pieces, mine, other):
            ks, vs = [], []
            for k, v, b in pieces:
                last = k.shape[0] - 1
                ks.append((k[:last] * mine).reshape(-1, LANES))
                ks.append(k[last] * mine + b * other)
                vs.append((v * mine + other).reshape(-1, LANES))
            return jnp.concatenate(ks, axis=0), jnp.concatenate(vs, axis=0)

        two, four = me // 2 * 2, me // 4 * 4
        small = segs * RUN
        lists = (
            (4, (
                keys(r16, two, 2, small, 0, 16, two + 1),
                keys(r8, two % 4, 2, small, 8, 16, two + 1),
                keys(r4, 0, 2, 2 * small, 4, 8, two + 1),
            )),
            (8, (
                keys(r16, four, 4, small, 0, 16, four + 3),
                keys(r8, 0, 4, small, 8, 16, four + 3),
            )),
            (16, (keys(r16, 0, n, small, 0, 16, n - 1),)),
        )
        for side in range(2):
            mine, other = sides[side]
            h = 2 * j + side
            for stride, pieces in lists:
                size = SEG0 // stride
                group = CLASSES // stride
                rows = rows_at(bitrev(h) // group * size, size)
                k, v = listed(pieces, mine, other)
                q = jnp.concatenate([qp[t, rows, here] for t in range(segs)], axis=0)
                acc, peak = attend(q * mine + other, k, v)
                for t in range(segs):
                    part = slice(t * size, (t + 1) * size)
                    acc_t, peak_t = merge(
                        acc_s[h, t, rows, :], peak_s[h, t, rows, :], acc[part], peak[part]
                    )
                    acc_s[h, t, rows, :] = acc_t
                    peak_s[h, t, rows, :] = peak_t
        wide = iota((SEG0, LANES), 1) < 64
        for t in range(segs):
            acc_e, acc_o = acc_s[2 * j, t], acc_s[2 * j + 1, t]
            total = pltpu.roll(jnp.where(wide, acc_o, acc_e), 64, 1)
            outp[t, :, here] = (jnp.where(wide, acc_e, acc_o) / total).astype(BF16)
        return 0

    lax.fori_loop(0, PAIRS, far, 0)

    back = jnp.where(new == (old % sub) * CLASSES + bitrev(old // sub), 1.0, 0.0).astype(BF16)

    def restore(step, _):
        lanes = pl.ds(pl.multiple_of(step * 256, 256), 256)
        for t in range(segs):
            for u in range(2):
                rows = jnp.concatenate(
                    [outp[t, pl.ds(i * RUN + u * sub, sub), lanes] for i in range(CLASSES)], axis=0
                )
                moved = jnp.dot(back, rows, preferred_element_type=F32)
                place = me * shard + t * SEG0 + u * half + iota((half, 256), 0)
                out_ref[pl.ds(t * SEG0 + u * half, half), lanes] = jnp.where(
                    place < length, moved, 0.0
                ).astype(BF16)
        return 0

    lax.fori_loop(0, WIDTH // 256, restore, 0)

    for c in first + second:
        c.wait_send()


def per_device(n, query_tiles, key_tiles, value_tiles, slide_length):
    shard = query_tiles.shape[0]
    segs = shard // SEG0
    chips = n // 2
    small = segs * RUN
    vmem = pl.BlockSpec(memory_space=pltpu.VMEM)
    dma = pltpu.SemaphoreType.DMA
    return pl.pallas_call(
        functools.partial(kernel, n),
        out_shape=jax.ShapeDtypeStruct((shard, WIDTH), BF16),
        in_specs=[pl.BlockSpec(memory_space=pltpu.SMEM), vmem, vmem, vmem],
        out_specs=vmem,
        scratch_shapes=[
            pltpu.VMEM((segs, SEG0, WIDTH), BF16),
            pltpu.VMEM((segs, SEG0, WIDTH), BF16),
            pltpu.VMEM((segs, SEG0, WIDTH), BF16),
            pltpu.VMEM((n, small, 2 * WIDTH), BF16),
            pltpu.VMEM((4, small, 2 * WIDTH), BF16),
            pltpu.VMEM((2, 2 * small, 2 * WIDTH), BF16),
            pltpu.VMEM((segs, SEG0, LANES), BF16),
            pltpu.VMEM((HEADS, segs, SEG0, LANES), F32),
            pltpu.VMEM((HEADS, segs, SEG0, LANES), F32),
            pltpu.VMEM((segs, SEG0, WIDTH), BF16),
            dma((chips,)), dma((n,)), dma((2,)), dma((4,)), dma((1,)), dma((2,)),
            dma((chips,)), dma((1,)),
        ],
        compiler_params=pltpu.CompilerParams(
            collective_id=0, has_side_effects=True, vmem_limit_bytes=56 * 1024 * 1024
        ),
        cost_estimate=pl.CostEstimate(
            flops=256 * shard * HEADS * 1024, bytes_accessed=8 * shard * WIDTH,
            transcendentals=shard * HEADS * 1024,
        ),
    )(slide_length, query_tiles, key_tiles, value_tiles)


def solution(mesh):
    placed = P(("slide", "seq"), None)
    return jax.shard_map(
        functools.partial(per_device, mesh.shape["seq"]),
        mesh=mesh,
        in_specs=(placed, placed, placed, P("slide")),
        out_specs=placed,
        check_vma=False,
    )
```

```python
import functools
import math

import jax
import jax.numpy as jnp
from jax import lax
from jax.experimental import pallas as pl
from jax.experimental.pallas import tpu as pltpu
from jax.sharding import PartitionSpec as P

HEADS = 12
WIDTH = 768
SEG0 = 512
CLASSES = 16
PAIRS = HEADS // 2
RUN = SEG0 // CLASSES
LANES = 128
MESH = pl.DeviceIdType.MESH
BF16 = jnp.bfloat16
F32 = jnp.float32
EXP_SCALE = 0.125 * math.log2(math.e)
MASK = -1e9


def bitrev(c):
    return (c % 2) * 8 + (c // 2 % 2) * 4 + (c // 4 % 2) * 2 + c // 8 % 2


def rows_at(start, size):
    return pl.ds(pl.multiple_of(start, RUN), size)


def pair_lanes(j, base=0):
    return pl.ds(pl.multiple_of(base + j * LANES, LANES), LANES)


def iota(shape, dim):
    return lax.broadcasted_iota(jnp.int32, shape, dim)


def staged(units):
    held = None
    for unit in units + [None]:
        ahead = None
        if unit is not None:
            q, k, v, take = unit
            scores = lax.dot_general(q, k, (((1,), (1,)), ((), ())), preferred_element_type=F32)
            ahead = (scores, v, take)
        if held is not None:
            scores, v, take = held
            peak = jnp.max(scores, axis=1, keepdims=True)
            weights = jnp.exp2((scores - peak) * EXP_SCALE).astype(BF16)
            take(jnp.dot(weights, v, preferred_element_type=F32), peak)
        held = ahead


def merge(acc, peak, acc_b, peak_b):
    top = jnp.maximum(peak, peak_b)
    keep = jnp.exp2((peak - top) * EXP_SCALE)
    add = jnp.exp2((peak_b - top) * EXP_SCALE)
    return acc * keep + acc_b * add, top


def kernel(
    n, len_ref, q_ref, k_ref, v_ref, out_ref,
    qp, kp, vp, r16, r8, r4, bias0, acc_s, peak_s, outp,
    send16, recv16, send8, recv8, send4, recv4, fwd16, fwd8,
):
    shard = q_ref.shape[0]
    segs = shard // SEG0
    chips = n // 2
    me = lax.axis_index("seq")
    chip, core = me // 2, me % 2
    sibling = chip * 2 + 1 - core
    mate_chip = chip + 1 - 2 * (chip % 2)
    mate = mate_chip * 2 + core
    length = len_ref[0]

    barrier = pltpu.get_barrier_semaphore()
    peers = [sibling] + [(chip + step) % chips * 2 + core for step in range(1, chips)]
    for peer in peers:
        pl.semaphore_signal(barrier, inc=1, device_id={"seq": peer}, device_id_type=MESH)

    half = SEG0 // 2
    sub = half // CLASSES
    new = iota((half, half), 0)
    old = iota((half, half), 1)
    shuffle = jnp.where(old == (new % sub) * CLASSES + bitrev(new // sub), 1.0, 0.0).astype(BF16)

    def permute(src, dst):
        def column(step, _):
            lanes = pl.ds(pl.multiple_of(step * 256, 256), 256)
            for t in range(segs):
                for u in range(2):
                    rows = src[pl.ds(t * SEG0 + u * half, half), lanes]
                    moved = jnp.dot(shuffle, rows, preferred_element_type=F32).astype(BF16)
                    for i in range(CLASSES):
                        dst[t, pl.ds(i * RUN + u * sub, sub), lanes] = moved[i * sub:(i + 1) * sub]
            return 0
        lax.fori_loop(0, WIDTH // 256, column, 0)

    permute(k_ref, kp)
    permute(v_ref, vp)

    lane = iota((1, LANES), 1)
    even = jnp.where(lane < 64, 1.0, 0.0).astype(BF16)
    odd = jnp.where(lane < 64, 0.0, 1.0).astype(BF16)
    sides = ((even, odd), (odd, even))

    def gather(j, _):
        for src, base in ((kp, 0), (vp, WIDTH)):
            here = pair_lanes(j)
            there = pair_lanes(j, base)
            for t in range(segs):
                def mixed(shift, keep, size):
                    e = src[t, rows_at(bitrev((2 * j + shift) % keep) * RUN, size), here]
                    o = src[t, rows_at(bitrev((2 * j + 1 + shift) % keep) * RUN, size), here]
                    return e * even + o * odd
                r16[me, pl.ds(t * RUN, RUN), there] = mixed(0, 16, RUN)
                r8[me % 4, pl.ds(t * RUN, RUN), there] = mixed(8, 16, RUN)
                r4[me % 2, pl.ds(t * 2 * RUN, 2 * RUN), there] = mixed(4, 8, 2 * RUN)
        return 0

    lax.fori_loop(0, PAIRS, gather, 0)

    pl.semaphore_wait(barrier, chips)

    def copy(buf, slot, send, recv, peer):
        return pltpu.make_async_remote_copy(
            src_ref=buf.at[slot], dst_ref=buf.at[slot], send_sem=send, recv_sem=recv.at[slot],
            device_id={"seq": peer}, device_id_type=MESH,
        )

    first = []
    for step in range(chips - 1, 0, -1):
        first.append(copy(r16, me, send16.at[step], recv16, (chip + step) % chips * 2 + core))
    first.append(copy(r8, me % 4, send8.at[1], recv8, mate))
    first.append(copy(r16, me, send16.at[0], recv16, sibling))
    first.append(copy(r8, me % 4, send8.at[0], recv8, sibling))
    first.append(copy(r4, me % 2, send4.at[0], recv4, sibling))
    for c in first:
        c.start()

    permute(q_ref, qp)

    row = iota((SEG0, LANES), 0)
    for t in range(segs):
        place = me * shard + t * SEG0 + (row % RUN) * CLASSES + bitrev(row // RUN)
        bias0[t] = jnp.where(place < length, 0.0, MASK).astype(BF16)

    def near(j, _):
        here = pair_lanes(j)
        units = []
        for side in range(2):
            mine, other = sides[side]
            h = 2 * j + side
            mid = pl.ds(side * half, half)
            low = pl.ds((1 - side) * half, half)

            def keys(t, rows):
                return kp[t, rows, here] * mine + bias0[t, rows, :] * other

            def values(t, rows):
                return vp[t, rows, here] * mine + other

            def query(t, rows):
                return qp[t, rows, here] * mine + other

            def keep_low(t, h=h, low=low):
                def take(acc, peak):
                    acc_s[h, t, low, :] = acc
                return take

            def keep_mid(t, h=h, mid=mid):
                def take(acc, peak):
                    acc_s[h, t, mid, :] = acc
                    peak_s[h, t] = jnp.broadcast_to(peak, (half, LANES))
                return take

            k_all = jnp.concatenate([keys(0, low), keys(0, mid), keys(1, mid), keys(1, low)], axis=0)
            low0, mid0, mid1, low1 = values(0, low), values(0, mid), values(1, mid), values(1, low)
            units += [
                (query(0, low), k_all[:2 * half], jnp.concatenate([low0, mid0], axis=0), keep_low(0)),
                (
                    query(0, mid), k_all[:3 * half],
                    jnp.concatenate([low0, mid0 + mid0, mid1], axis=0), keep_mid(0),
                ),
                (
                    query(1, mid), k_all[half:],
                    jnp.concatenate([mid0, mid1 + mid1, low1], axis=0), keep_mid(1),
                ),
                (query(1, low), k_all[2 * half:], jnp.concatenate([mid1, low1], axis=0), keep_low(1)),
            ]
        staged(units)
        return 0

    split = 4
    lax.fori_loop(0, split, near, 0)

    second = []
    for step in range(1, chips):
        source = (chip + chips - step) % chips * 2 + core
        copy(r16, source, send16.at[step], recv16, sibling).wait_recv()
        c = copy(r16, source, fwd16.at[step], recv16, sibling)
        c.start()
        second.append(c)
    copy(r8, mate % 4, send8.at[1], recv8, sibling).wait_recv()
    c = copy(r8, mate % 4, fwd8.at[0], recv8, sibling)
    c.start()
    second.append(c)

    lax.fori_loop(split, PAIRS, near, 0)

    copy(r16, sibling, send16.at[0], recv16, sibling).wait_recv()
    copy(r8, sibling % 4, send8.at[0], recv8, sibling).wait_recv()
    copy(r4, sibling % 2, send4.at[0], recv4, sibling).wait_recv()
    for step in range(1, chips):
        source = (chip + chips - step) % chips * 2 + 1 - core
        copy(r16, source, fwd16.at[step], recv16, sibling).wait_recv()
    far_mate = mate_chip * 2 + 1 - core
    copy(r8, far_mate % 4, fwd8.at[0], recv8, sibling).wait_recv()

    head_lane = 1 - iota((1, LANES), 1) // 64

    def far(j, _):
        here = pair_lanes(j)
        there = pair_lanes(j, WIDTH)
        heads = 2 * j + head_lane

        def bias(slot, size, shift, keep):
            r = iota((size, LANES), 0)
            width = size // segs
            inner = r % width
            place = (
                slot * shard + r // width * SEG0 + inner % RUN * CLASSES
                + inner // RUN * 8 + (heads + shift) % keep
            )
            return jnp.where(place < length, 0.0, MASK).astype(BF16)

        def keys(buf, start, count, size, shift, keep, owner):
            k = buf[pl.ds(start, count), :, here]
            v = buf[pl.ds(start, count), :, there]
            return k, v, bias(owner, size, shift, keep)

        def listed(pieces, mine, other):
            ks, vs = [], []
            for k, v, b in pieces:
                last = k.shape[0] - 1
                ks.append((k[:last] * mine).reshape(-1, LANES))
                ks.append(k[last] * mine + b * other)
                vs.append((v * mine + other).reshape(-1, LANES))
            return jnp.concatenate(ks, axis=0), jnp.concatenate(vs, axis=0)

        two, four = me // 2 * 2, me // 4 * 4
        small = segs * RUN
        lists = (
            (4, (
                keys(r16, two, 2, small, 0, 16, two + 1),
                keys(r8, two % 4, 2, small, 8, 16, two + 1),
                keys(r4, 0, 2, 2 * small, 4, 8, two + 1),
            )),
            (8, (
                keys(r16, four, 4, small, 0, 16, four + 3),
                keys(r8, 0, 4, small, 8, 16, four + 3),
            )),
            (16, (keys(r16, 0, n, small, 0, 16, n - 1),)),
        )
        units = []
        for side in range(2):
            mine, other = sides[side]
            h = 2 * j + side
            for stride, pieces in lists:
                size = SEG0 // stride
                group = CLASSES // stride
                start = bitrev(h) // group * size
                k, v = listed(pieces, mine, other)
                q = jnp.concatenate([qp[t, rows_at(start, size), here] for t in range(segs)], axis=0)

                def take(acc, peak, h=h, start=start, size=size, side=side):
                    rows = rows_at(start, size)
                    inner = rows_at(start - side * half, size)
                    for t in range(segs):
                        part = slice(t * size, (t + 1) * size)
                        acc_t, peak_t = merge(
                            acc_s[h, t, rows, :], peak_s[h, t, inner, :], acc[part], peak[part]
                        )
                        acc_s[h, t, rows, :] = acc_t
                        peak_s[h, t, inner, :] = peak_t

                units.append((q * mine + other, k, v, take))
        staged(units)
        wide = iota((SEG0, LANES), 1) < 64
        for t in range(segs):
            acc_e, acc_o = acc_s[2 * j, t], acc_s[2 * j + 1, t]
            total = pltpu.roll(jnp.where(wide, acc_o, acc_e), 64, 1)
            outp[t, :, here] = (jnp.where(wide, acc_e, acc_o) / total).astype(BF16)
        return 0

    lax.fori_loop(0, PAIRS, far, 0)

    back = jnp.where(new == (old % sub) * CLASSES + bitrev(old // sub), 1.0, 0.0).astype(BF16)

    def restore(step, _):
        lanes = pl.ds(pl.multiple_of(step * 256, 256), 256)
        for t in range(segs):
            for u in range(2):
                rows = jnp.concatenate(
                    [outp[t, pl.ds(i * RUN + u * sub, sub), lanes] for i in range(CLASSES)], axis=0
                )
                moved = jnp.dot(back, rows, preferred_element_type=F32)
                place = me * shard + t * SEG0 + u * half + iota((half, 256), 0)
                out_ref[pl.ds(t * SEG0 + u * half, half), lanes] = jnp.where(
                    place < length, moved, 0.0
                ).astype(BF16)
        return 0

    lax.fori_loop(0, WIDTH // 256, restore, 0)

    for c in first + second:
        c.wait_send()


def per_device(n, query_tiles, key_tiles, value_tiles, slide_length):
    shard = query_tiles.shape[0]
    segs = shard // SEG0
    chips = n // 2
    small = segs * RUN
    vmem = pl.BlockSpec(memory_space=pltpu.VMEM)
    dma = pltpu.SemaphoreType.DMA
    return pl.pallas_call(
        functools.partial(kernel, n),
        out_shape=jax.ShapeDtypeStruct((shard, WIDTH), BF16),
        in_specs=[pl.BlockSpec(memory_space=pltpu.SMEM), vmem, vmem, vmem],
        out_specs=vmem,
        scratch_shapes=[
            pltpu.VMEM((segs, SEG0, WIDTH), BF16),
            pltpu.VMEM((segs, SEG0, WIDTH), BF16),
            pltpu.VMEM((segs, SEG0, WIDTH), BF16),
            pltpu.VMEM((n, small, 2 * WIDTH), BF16),
            pltpu.VMEM((4, small, 2 * WIDTH), BF16),
            pltpu.VMEM((2, 2 * small, 2 * WIDTH), BF16),
            pltpu.VMEM((segs, SEG0, LANES), BF16),
            pltpu.VMEM((HEADS, segs, SEG0, LANES), F32),
            pltpu.VMEM((HEADS, segs, SEG0 // 2, LANES), F32),
            pltpu.VMEM((segs, SEG0, WIDTH), BF16),
            dma((chips,)), dma((n,)), dma((2,)), dma((4,)), dma((1,)), dma((2,)),
            dma((chips,)), dma((1,)),
        ],
        compiler_params=pltpu.CompilerParams(
            collective_id=0, has_side_effects=True, vmem_limit_bytes=56 * 1024 * 1024
        ),
        cost_estimate=pl.CostEstimate(
            flops=256 * shard * HEADS * 1024, bytes_accessed=8 * shard * WIDTH,
            transcendentals=shard * HEADS * 1024,
        ),
    )(slide_length, query_tiles, key_tiles, value_tiles)


def solution(mesh):
    placed = P(("slide", "seq"), None)
    return jax.shard_map(
        functools.partial(per_device, mesh.shape["seq"]),
        mesh=mesh,
        in_specs=(placed, placed, placed, P("slide")),
        out_specs=placed,
        check_vma=False,
    )
```

```python
import functools
import math

import jax
import jax.numpy as jnp
from jax import lax
from jax.experimental import pallas as pl
from jax.experimental.pallas import tpu as pltpu
from jax.sharding import PartitionSpec as P

HEADS = 12
WIDTH = 768
SEG0 = 512
CLASSES = 16
PAIRS = HEADS // 2
RUN = SEG0 // CLASSES
LANES = 128
MESH = pl.DeviceIdType.MESH
BF16 = jnp.bfloat16
F32 = jnp.float32
EXP_SCALE = 0.125 * math.log2(math.e)
MASK = -1e9


def bitrev(c):
    return (c % 2) * 8 + (c // 2 % 2) * 4 + (c // 4 % 2) * 2 + c // 8 % 2


def rows_at(start, size):
    return pl.ds(pl.multiple_of(start, RUN), size)


def pair_lanes(j, base=0):
    return pl.ds(pl.multiple_of(base + j * LANES, LANES), LANES)


def iota(shape, dim):
    return lax.broadcasted_iota(jnp.int32, shape, dim)


def staged(units):
    held = None
    for unit in units + [None]:
        ahead = None
        if unit is not None:
            q, k, v, take = unit
            scores = jnp.dot(q, k, preferred_element_type=F32)
            ahead = (scores, v, take)
        if held is not None:
            scores, v, take = held
            columns = [scores[:, at:at + LANES] for at in range(0, scores.shape[1], LANES)]
            peak = jnp.max(functools.reduce(jnp.maximum, columns), axis=1, keepdims=True)
            weights = jnp.exp2((scores - peak) * EXP_SCALE).astype(BF16)
            take(jnp.dot(weights, v, preferred_element_type=F32), peak)
        held = ahead


def merge(acc, peak, acc_b, peak_b):
    top = jnp.maximum(peak, peak_b)
    keep = jnp.exp2((peak - top) * EXP_SCALE)
    add = jnp.exp2((peak_b - top) * EXP_SCALE)
    return acc * keep + acc_b * add, top


def kernel(
    n, len_ref, q_ref, k_ref, v_ref, out_ref,
    qp, kp, vp, r16, r8, r4, bias0, acc_s, peak_s, outp,
    send16, recv16, send8, recv8, send4, recv4, fwd16, fwd8,
):
    shard = q_ref.shape[0]
    segs = shard // SEG0
    chips = n // 2
    me = lax.axis_index("seq")
    chip, core = me // 2, me % 2
    sibling = chip * 2 + 1 - core
    mate_chip = chip + 1 - 2 * (chip % 2)
    mate = mate_chip * 2 + core
    length = len_ref[0]

    barrier = pltpu.get_barrier_semaphore()
    peers = [sibling] + [(chip + step) % chips * 2 + core for step in range(1, chips)]
    for peer in peers:
        pl.semaphore_signal(barrier, inc=1, device_id={"seq": peer}, device_id_type=MESH)

    half = SEG0 // 2
    sub = half // CLASSES
    new = iota((half, half), 0)
    old = iota((half, half), 1)
    shuffle = jnp.where(old == (new % sub) * CLASSES + bitrev(new // sub), 1.0, 0.0).astype(BF16)

    def permute(src, dst):
        def column(step, _):
            lanes = pl.ds(pl.multiple_of(step * 256, 256), 256)
            for t in range(segs):
                for u in range(2):
                    rows = src[pl.ds(t * SEG0 + u * half, half), lanes]
                    moved = jnp.dot(shuffle, rows, preferred_element_type=F32).astype(BF16)
                    for i in range(CLASSES):
                        dst[t, pl.ds(i * RUN + u * sub, sub), lanes] = moved[i * sub:(i + 1) * sub]
            return 0
        lax.fori_loop(0, WIDTH // 256, column, 0)

    permute(k_ref, kp)
    permute(v_ref, vp)

    lane = iota((1, LANES), 1)
    even = jnp.where(lane < 64, 1.0, 0.0).astype(BF16)
    odd = jnp.where(lane < 64, 0.0, 1.0).astype(BF16)
    sides = ((even, odd), (odd, even))

    def gather(j, _):
        for src, base in ((kp, 0), (vp, WIDTH)):
            here = pair_lanes(j)
            there = pair_lanes(j, base)
            for t in range(segs):
                def mixed(shift, keep, size):
                    e = src[t, rows_at(bitrev((2 * j + shift) % keep) * RUN, size), here]
                    o = src[t, rows_at(bitrev((2 * j + 1 + shift) % keep) * RUN, size), here]
                    return e * even + o * odd
                r16[me, pl.ds(t * RUN, RUN), there] = mixed(0, 16, RUN)
                r8[me % 4, pl.ds(t * RUN, RUN), there] = mixed(8, 16, RUN)
                r4[me % 2, pl.ds(t * 2 * RUN, 2 * RUN), there] = mixed(4, 8, 2 * RUN)
        return 0

    lax.fori_loop(0, PAIRS, gather, 0)

    pl.semaphore_wait(barrier, chips)

    def copy(buf, slot, send, recv, peer):
        return pltpu.make_async_remote_copy(
            src_ref=buf.at[slot], dst_ref=buf.at[slot], send_sem=send, recv_sem=recv.at[slot],
            device_id={"seq": peer}, device_id_type=MESH,
        )

    first = []
    for step in range(chips - 1, 0, -1):
        first.append(copy(r16, me, send16.at[step], recv16, (chip + step) % chips * 2 + core))
    first.append(copy(r8, me % 4, send8.at[1], recv8, mate))
    first.append(copy(r16, me, send16.at[0], recv16, sibling))
    first.append(copy(r8, me % 4, send8.at[0], recv8, sibling))
    first.append(copy(r4, me % 2, send4.at[0], recv4, sibling))
    for c in first:
        c.start()

    permute(q_ref, qp)

    def bias_rows(place):
        fill = jnp.where(place < length, 0.0, MASK)
        return jnp.broadcast_to(fill, (LANES // 2, fill.shape[1])).astype(BF16)

    def one_head(kt, fill, side):
        mine = kt[side * 64:side * 64 + 64]
        return jnp.concatenate([fill, mine] if side else [mine, fill], axis=0)

    column = iota((1, SEG0), 1)
    for t in range(segs):
        place = me * shard + t * SEG0 + (column % RUN) * CLASSES + bitrev(column // RUN)
        bias0[t] = bias_rows(place)

    def near(j, _):
        here = pair_lanes(j)
        units = []
        kt = [jnp.transpose(kp[t, :, here]) for t in range(segs)]
        for side in range(2):
            mine, other = sides[side]
            h = 2 * j + side
            mid = pl.ds(side * half, half)
            low = pl.ds((1 - side) * half, half)

            full = [one_head(kt[t], bias0[t], side) for t in range(segs)]

            def keys(t, mid_rows):
                at = half if bool(side) == mid_rows else 0
                return full[t][:, at:at + half]

            def values(t, rows):
                return vp[t, rows, here] * mine + other

            def query(t, rows):
                return qp[t, rows, here] * mine + other

            def keep_low(t, h=h, low=low):
                def take(acc, peak):
                    acc_s[h, t, low, :] = acc
                return take

            def keep_mid(t, h=h, mid=mid):
                def take(acc, peak):
                    acc_s[h, t, mid, :] = acc
                    peak_s[h, t] = jnp.broadcast_to(peak, (half, LANES))
                return take

            k_all = jnp.concatenate(
                [keys(0, False), keys(0, True), keys(1, True), keys(1, False)], axis=1
            )
            low0, mid0, mid1, low1 = values(0, low), values(0, mid), values(1, mid), values(1, low)
            units += [
                (query(0, low), k_all[:, :2 * half], jnp.concatenate([low0, mid0], axis=0), keep_low(0)),
                (
                    query(0, mid), k_all[:, :3 * half],
                    jnp.concatenate([low0, mid0 + mid0, mid1], axis=0), keep_mid(0),
                ),
                (
                    query(1, mid), k_all[:, half:],
                    jnp.concatenate([mid0, mid1 + mid1, low1], axis=0), keep_mid(1),
                ),
                (query(1, low), k_all[:, 2 * half:], jnp.concatenate([mid1, low1], axis=0), keep_low(1)),
            ]
        staged(units)
        return 0

    split = 4
    lax.fori_loop(0, split, near, 0)

    second = []
    for step in range(1, chips):
        source = (chip + chips - step) % chips * 2 + core
        copy(r16, source, send16.at[step], recv16, sibling).wait_recv()
        c = copy(r16, source, fwd16.at[step], recv16, sibling)
        c.start()
        second.append(c)
    copy(r8, mate % 4, send8.at[1], recv8, sibling).wait_recv()
    c = copy(r8, mate % 4, fwd8.at[0], recv8, sibling)
    c.start()
    second.append(c)

    lax.fori_loop(split, PAIRS, near, 0)

    copy(r16, sibling, send16.at[0], recv16, sibling).wait_recv()
    copy(r8, sibling % 4, send8.at[0], recv8, sibling).wait_recv()
    copy(r4, sibling % 2, send4.at[0], recv4, sibling).wait_recv()
    for step in range(1, chips):
        source = (chip + chips - step) % chips * 2 + 1 - core
        copy(r16, source, fwd16.at[step], recv16, sibling).wait_recv()
    far_mate = mate_chip * 2 + 1 - core
    copy(r8, far_mate % 4, fwd8.at[0], recv8, sibling).wait_recv()

    def far(j, _):
        here = pair_lanes(j)
        there = pair_lanes(j, WIDTH)

        def piece(buf, start, count, shift, keep, owner):
            size = buf.shape[1]
            width = size // segs
            r = iota((1, count * size), 1)
            inner = r % width
            place = (
                (owner + r // size) * shard + r % size // width * SEG0
                + inner % RUN * CLASSES + inner // RUN * 8
            )
            k = buf[pl.ds(start, count), :, here].reshape(-1, LANES)
            v = buf[pl.ds(start, count), :, there].reshape(-1, LANES)
            return k, v, place, shift, keep

        def listed(pieces):
            k = jnp.concatenate([p[0] for p in pieces], axis=0)
            v = jnp.concatenate([p[1] for p in pieces], axis=0)
            return jnp.transpose(k), v, [p[2:] for p in pieces]

        two, four = me // 2 * 2, me // 4 * 4
        lists = (
            (4, listed((
                piece(r16, two, 2, 0, 16, two),
                piece(r8, two % 4, 2, 8, 16, two),
                piece(r4, 0, 2, 4, 8, two),
            ))),
            (8, listed((piece(r16, four, 4, 0, 16, four), piece(r8, 0, 4, 8, 16, four)))),
            (16, listed((piece(r16, 0, n, 0, 16, 0),))),
        )
        units = []
        for side in range(2):
            mine, other = sides[side]
            h = 2 * j + side
            for stride, (kt, values, places) in lists:
                size = SEG0 // stride
                group = CLASSES // stride
                start = bitrev(h) // group * size
                fill = jnp.concatenate(
                    [bias_rows(place + (h + shift) % keep) for place, shift, keep in places], axis=1
                )
                k, v = one_head(kt, fill, side), values * mine + other
                q = jnp.concatenate([qp[t, rows_at(start, size), here] for t in range(segs)], axis=0)

                def take(acc, peak, h=h, start=start, size=size, side=side):
                    rows = rows_at(start, size)
                    inner = rows_at(start - side * half, size)
                    for t in range(segs):
                        part = slice(t * size, (t + 1) * size)
                        acc_t, peak_t = merge(
                            acc_s[h, t, rows, :], peak_s[h, t, inner, :], acc[part], peak[part]
                        )
                        acc_s[h, t, rows, :] = acc_t
                        peak_s[h, t, inner, :] = peak_t

                units.append((q * mine + other, k, v, take))
        staged(units)
        wide = iota((SEG0, LANES), 1) < 64
        for t in range(segs):
            acc_e, acc_o = acc_s[2 * j, t], acc_s[2 * j + 1, t]
            total = pltpu.roll(jnp.where(wide, acc_o, acc_e), 64, 1)
            outp[t, :, here] = (jnp.where(wide, acc_e, acc_o) / total).astype(BF16)
        return 0

    lax.fori_loop(0, PAIRS, far, 0)

    back = jnp.where(new == (old % sub) * CLASSES + bitrev(old // sub), 1.0, 0.0).astype(BF16)

    def restore(step, _):
        lanes = pl.ds(pl.multiple_of(step * 256, 256), 256)
        for t in range(segs):
            for u in range(2):
                rows = jnp.concatenate(
                    [outp[t, pl.ds(i * RUN + u * sub, sub), lanes] for i in range(CLASSES)], axis=0
                )
                moved = jnp.dot(back, rows, preferred_element_type=F32)
                place = me * shard + t * SEG0 + u * half + iota((half, 256), 0)
                out_ref[pl.ds(t * SEG0 + u * half, half), lanes] = jnp.where(
                    place < length, moved, 0.0
                ).astype(BF16)
        return 0

    lax.fori_loop(0, WIDTH // 256, restore, 0)

    for c in first + second:
        c.wait_send()


def per_device(n, query_tiles, key_tiles, value_tiles, slide_length):
    shard = query_tiles.shape[0]
    segs = shard // SEG0
    chips = n // 2
    small = segs * RUN
    vmem = pl.BlockSpec(memory_space=pltpu.VMEM)
    dma = pltpu.SemaphoreType.DMA
    return pl.pallas_call(
        functools.partial(kernel, n),
        out_shape=jax.ShapeDtypeStruct((shard, WIDTH), BF16),
        in_specs=[pl.BlockSpec(memory_space=pltpu.SMEM), vmem, vmem, vmem],
        out_specs=vmem,
        scratch_shapes=[
            pltpu.VMEM((segs, SEG0, WIDTH), BF16),
            pltpu.VMEM((segs, SEG0, WIDTH), BF16),
            pltpu.VMEM((segs, SEG0, WIDTH), BF16),
            pltpu.VMEM((n, small, 2 * WIDTH), BF16),
            pltpu.VMEM((4, small, 2 * WIDTH), BF16),
            pltpu.VMEM((2, 2 * small, 2 * WIDTH), BF16),
            pltpu.VMEM((segs, LANES // 2, SEG0), BF16),
            pltpu.VMEM((HEADS, segs, SEG0, LANES), F32),
            pltpu.VMEM((HEADS, segs, SEG0 // 2, LANES), F32),
            pltpu.VMEM((segs, SEG0, WIDTH), BF16),
            dma((chips,)), dma((n,)), dma((2,)), dma((4,)), dma((1,)), dma((2,)),
            dma((chips,)), dma((1,)),
        ],
        compiler_params=pltpu.CompilerParams(
            collective_id=0, has_side_effects=True, vmem_limit_bytes=56 * 1024 * 1024
        ),
        cost_estimate=pl.CostEstimate(
            flops=256 * shard * HEADS * 1024, bytes_accessed=8 * shard * WIDTH,
            transcendentals=shard * HEADS * 1024,
        ),
    )(slide_length, query_tiles, key_tiles, value_tiles)


def solution(mesh):
    placed = P(("slide", "seq"), None)
    return jax.shard_map(
        functools.partial(per_device, mesh.shape["seq"]),
        mesh=mesh,
        in_specs=(placed, placed, placed, P("slide")),
        out_specs=placed,
        check_vma=False,
    )
```

```python
import functools
import math

import jax
import jax.numpy as jnp
from jax import lax
from jax.experimental import pallas as pl
from jax.experimental.pallas import tpu as pltpu
from jax.sharding import PartitionSpec as P

HEADS = 12
WIDTH = 768
SEG0 = 512
CLASSES = 16
PAIRS = HEADS // 2
RUN = SEG0 // CLASSES
LANES = 128
MESH = pl.DeviceIdType.MESH
BF16 = jnp.bfloat16
F32 = jnp.float32
EXP_SCALE = 0.125 * math.log2(math.e)
MASK = -1e9


def bitrev(c):
    return ((c & 1) << 3) + ((c & 2) << 1) + ((c & 4) >> 1) + ((c & 8) >> 3)


def home(j, side):
    return 8 * side + lax.rem(j, 2) * 4 + lax.rem(lax.div(j, 2), 2) * 2 + lax.div(j, 4)


def rows_at(start, size):
    return pl.ds(pl.multiple_of(start, RUN), size)


def pair_lanes(j, base=0):
    return pl.ds(pl.multiple_of(base + j * LANES, LANES), LANES)


def iota(shape, dim):
    return lax.broadcasted_iota(jnp.int32, shape, dim)


def staged(units):
    held = None
    for unit in units + [None]:
        ahead = None
        if unit is not None:
            q, k, v, take = unit
            scores = jnp.dot(q, k, preferred_element_type=F32)
            ahead = (scores, v, take)
        if held is not None:
            scores, v, take = held
            columns = [scores[:, at:at + LANES] for at in range(0, scores.shape[1], LANES)]
            peak = jnp.max(functools.reduce(jnp.maximum, columns), axis=1, keepdims=True)
            weights = jnp.exp2((scores - peak) * EXP_SCALE).astype(BF16)
            take(jnp.dot(weights, v, preferred_element_type=F32), peak)
        held = ahead


def merge(acc, peak, acc_b, peak_b):
    top = jnp.maximum(peak, peak_b)
    keep = jnp.exp2((peak - top) * EXP_SCALE)
    add = jnp.exp2((peak_b - top) * EXP_SCALE)
    return acc * keep + acc_b * add, top


def kernel(
    n, len_ref, q_ref, k_ref, v_ref, out_ref,
    qp, kp, vp, r16, r8, r4, bias0, acc_s, peak_s, outp,
    send16, recv16, send8, recv8, send4, recv4, fwd16, fwd8,
):
    shard = q_ref.shape[0]
    segs = shard // SEG0
    chips = n // 2
    me = lax.axis_index("seq")
    chip, core = me // 2, me % 2
    sibling = chip * 2 + 1 - core
    mate_chip = chip + 1 - 2 * (chip % 2)
    mate = mate_chip * 2 + core
    length = len_ref[0]

    barrier = pltpu.get_barrier_semaphore()
    peers = [sibling] + [(chip + step) % chips * 2 + core for step in range(1, chips)]
    for peer in peers:
        pl.semaphore_signal(barrier, inc=1, device_id={"seq": peer}, device_id_type=MESH)

    half = SEG0 // 2
    sub = half // CLASSES
    new = iota((half, half), 0)
    old = iota((half, half), 1)
    shuffle = jnp.where(old == ((new & (sub - 1)) << 4) + bitrev(new >> 4), 1.0, 0.0).astype(BF16)

    def permute(src, dst):
        def column(step, _):
            lanes = pl.ds(pl.multiple_of(step * 256, 256), 256)
            for t in range(segs):
                for u in range(2):
                    rows = src[pl.ds(t * SEG0 + u * half, half), lanes]
                    moved = jnp.dot(shuffle, rows, preferred_element_type=F32).astype(BF16)
                    for i in range(CLASSES):
                        dst[t, pl.ds(i * RUN + u * sub, sub), lanes] = moved[i * sub:(i + 1) * sub]
            return 0
        lax.fori_loop(0, WIDTH // 256, column, 0)

    permute(k_ref, kp)
    permute(v_ref, vp)

    lane = iota((1, LANES), 1)
    even = jnp.where(lane < 64, 1.0, 0.0).astype(BF16)
    odd = jnp.where(lane < 64, 0.0, 1.0).astype(BF16)
    sides = ((even, odd), (odd, even))

    def gather(j, _):
        for src, base in ((kp, 0), (vp, WIDTH)):
            here = pair_lanes(j)
            there = pair_lanes(j, base)
            for t in range(segs):
                def mixed(turn, size):
                    e = src[t, rows_at(turn(home(j, 0)) * RUN, size), here]
                    o = src[t, rows_at(turn(home(j, 1)) * RUN, size), here]
                    return e * even + o * odd
                r16[me, pl.ds(t * RUN, RUN), there] = mixed(lambda c: c, RUN)
                r8[me % 4, pl.ds(t * RUN, RUN), there] = mixed(lambda c: c + 1 - 2 * lax.rem(c, 2), RUN)
                r4[me % 2, pl.ds(t * 2 * RUN, 2 * RUN), there] = mixed(lambda c: lax.div(c, 4) * 4 + 2 - lax.div(lax.rem(c, 4), 2) * 2, 2 * RUN)
        return 0

    lax.fori_loop(0, PAIRS, gather, 0)

    pl.semaphore_wait(barrier, chips)

    def copy(buf, slot, send, recv, peer):
        return pltpu.make_async_remote_copy(
            src_ref=buf.at[slot], dst_ref=buf.at[slot], send_sem=send, recv_sem=recv.at[slot],
            device_id={"seq": peer}, device_id_type=MESH,
        )

    first = []
    for step in range(chips - 1, 0, -1):
        first.append(copy(r16, me, send16.at[step], recv16, (chip + step) % chips * 2 + core))
    first.append(copy(r8, me % 4, send8.at[1], recv8, mate))
    first.append(copy(r16, me, send16.at[0], recv16, sibling))
    first.append(copy(r8, me % 4, send8.at[0], recv8, sibling))
    first.append(copy(r4, me % 2, send4.at[0], recv4, sibling))
    for c in first:
        c.start()

    permute(q_ref, qp)

    def bias_rows(place):
        fill = jnp.where(place < length, 0.0, MASK)
        return jnp.broadcast_to(fill, (LANES // 2, fill.shape[1])).astype(BF16)

    def one_head(kt, fill, side):
        mine = kt[side * 64:side * 64 + 64]
        return jnp.concatenate([fill, mine] if side else [mine, fill], axis=0)

    column = iota((1, SEG0), 1)
    for t in range(segs):
        place = me * shard + t * SEG0 + ((column & (RUN - 1)) << 4) + bitrev(column >> 5)
        bias0[t] = bias_rows(place)

    def near(j, _):
        here = pair_lanes(j)
        units = []
        kt = [jnp.transpose(kp[t, :, here]) for t in range(segs)]
        for side in range(2):
            mine, other = sides[side]
            h = 2 * j + side
            mid = pl.ds(side * half, half)
            low = pl.ds((1 - side) * half, half)

            full = [one_head(kt[t], bias0[t], side) for t in range(segs)]

            def keys(t, mid_rows):
                at = half if bool(side) == mid_rows else 0
                return full[t][:, at:at + half]

            def values(t, rows):
                return vp[t, rows, here] * mine + other

            def query(t, rows):
                return qp[t, rows, here] * mine + other

            def keep_low(t, h=h, low=low):
                def take(acc, peak):
                    acc_s[h, t, low, :] = acc
                return take

            def keep_mid(t, h=h, mid=mid):
                def take(acc, peak):
                    acc_s[h, t, mid, :] = acc
                    peak_s[h, t] = jnp.broadcast_to(peak, (half, LANES))
                return take

            k_all = jnp.concatenate(
                [keys(0, False), keys(0, True), keys(1, True), keys(1, False)], axis=1
            )
            low0, mid0, mid1, low1 = values(0, low), values(0, mid), values(1, mid), values(1, low)
            units += [
                (query(0, low), k_all[:, :2 * half], jnp.concatenate([low0, mid0], axis=0), keep_low(0)),
                (
                    query(0, mid), k_all[:, :3 * half],
                    jnp.concatenate([low0, mid0 + mid0, mid1], axis=0), keep_mid(0),
                ),
                (
                    query(1, mid), k_all[:, half:],
                    jnp.concatenate([mid0, mid1 + mid1, low1], axis=0), keep_mid(1),
                ),
                (query(1, low), k_all[:, 2 * half:], jnp.concatenate([mid1, low1], axis=0), keep_low(1)),
            ]
        staged(units)
        return 0

    lax.fori_loop(0, PAIRS, near, 0)

    second = []
    for step in range(1, chips):
        source = (chip + chips - step) % chips * 2 + core
        copy(r16, source, send16.at[step], recv16, sibling).wait_recv()
        c = copy(r16, source, fwd16.at[step], recv16, sibling)
        c.start()
        second.append(c)
    copy(r8, mate % 4, send8.at[1], recv8, sibling).wait_recv()
    c = copy(r8, mate % 4, fwd8.at[0], recv8, sibling)
    c.start()
    second.append(c)

    copy(r16, sibling, send16.at[0], recv16, sibling).wait_recv()
    copy(r8, sibling % 4, send8.at[0], recv8, sibling).wait_recv()
    copy(r4, sibling % 2, send4.at[0], recv4, sibling).wait_recv()
    def far(strides, j, _):
        here = pair_lanes(j)
        there = pair_lanes(j, WIDTH)

        def piece(buf, start, count, shift, keep, owner):
            size = buf.shape[1]
            bits = size.bit_length() - 1
            r = iota((1, count * size), 1)
            place = (
                (owner + (r >> bits)) * shard + ((r >> (bits - 1)) & 1) * SEG0
                + ((r & (RUN - 1)) << 4)
            )
            if size > segs * RUN:
                place = place + ((r >> 5) & 1) * 8
            k = buf[pl.ds(start, count), :, here].reshape(-1, LANES)
            v = buf[pl.ds(start, count), :, there].reshape(-1, LANES)
            return k, v, place, shift, keep

        def listed(pieces):
            k = jnp.concatenate([p[0] for p in pieces], axis=0)
            v = jnp.concatenate([p[1] for p in pieces], axis=0)
            return jnp.transpose(k), v, [p[2:] for p in pieces]

        two, four = me // 2 * 2, me // 4 * 4
        lists = []
        if 4 in strides:
            lists.append((4, listed((
                piece(r16, two, 2, 0, 16, two),
                piece(r8, two % 4, 2, 8, 16, two),
                piece(r4, 0, 2, 4, 8, two),
            ))))
        if 8 in strides:
            lists.append((8, listed((
                piece(r16, four, 4, 0, 16, four), piece(r8, 0, 4, 8, 16, four),
            ))))
        if 16 in strides:
            lists.append((16, listed((piece(r16, 0, n, 0, 16, 0),))))
        units = []
        for side in range(2):
            mine, other = sides[side]
            h = 2 * j + side
            for stride, (kt, values, places) in lists:
                size = SEG0 // stride
                group = CLASSES // stride
                start = lax.div(home(j, side), group) * size
                fill = jnp.concatenate(
                    [bias_rows(place + ((h + shift) & (keep - 1))) for place, shift, keep in places], axis=1
                )
                k, v = one_head(kt, fill, side), values * mine + other
                q = jnp.concatenate([qp[t, rows_at(start, size), here] for t in range(segs)], axis=0)

                def take(acc, peak, h=h, start=start, size=size, side=side):
                    rows = rows_at(start, size)
                    inner = rows_at(start - side * half, size)
                    for t in range(segs):
                        part = slice(t * size, (t + 1) * size)
                        acc_t, peak_t = merge(
                            acc_s[h, t, rows, :], peak_s[h, t, inner, :], acc[part], peak[part]
                        )
                        acc_s[h, t, rows, :] = acc_t
                        peak_s[h, t, inner, :] = peak_t

                units.append((q * mine + other, k, v, take))
        staged(units)
        if 16 not in strides:
            return 0
        wide = iota((SEG0, LANES), 1) < 64
        for t in range(segs):
            acc_e, acc_o = acc_s[2 * j, t], acc_s[2 * j + 1, t]
            total = pltpu.roll(jnp.where(wide, acc_o, acc_e), 64, 1)
            outp[t, :, here] = (jnp.where(wide, acc_e, acc_o) / total).astype(BF16)
        return 0

    lax.fori_loop(0, PAIRS, functools.partial(far, (4,)), 0)

    for step in range(1, chips):
        source = (chip + chips - step) % chips * 2 + 1 - core
        copy(r16, source, fwd16.at[step], recv16, sibling).wait_recv()
    far_mate = mate_chip * 2 + 1 - core
    copy(r8, far_mate % 4, fwd8.at[0], recv8, sibling).wait_recv()

    lax.fori_loop(0, PAIRS, functools.partial(far, (8, 16)), 0)

    back = jnp.where(new == ((old & (sub - 1)) << 4) + bitrev(old >> 4), 1.0, 0.0).astype(BF16)

    def restore(step, _):
        lanes = pl.ds(pl.multiple_of(step * 256, 256), 256)
        for t in range(segs):
            for u in range(2):
                rows = jnp.concatenate(
                    [outp[t, pl.ds(i * RUN + u * sub, sub), lanes] for i in range(CLASSES)], axis=0
                )
                moved = jnp.dot(back, rows, preferred_element_type=F32)
                place = me * shard + t * SEG0 + u * half + iota((half, 256), 0)
                out_ref[pl.ds(t * SEG0 + u * half, half), lanes] = jnp.where(
                    place < length, moved, 0.0
                ).astype(BF16)
        return 0

    lax.fori_loop(0, WIDTH // 256, restore, 0)

    for c in first + second:
        c.wait_send()


def per_device(n, query_tiles, key_tiles, value_tiles, slide_length):
    shard = query_tiles.shape[0]
    segs = shard // SEG0
    chips = n // 2
    small = segs * RUN
    vmem = pl.BlockSpec(memory_space=pltpu.VMEM)
    dma = pltpu.SemaphoreType.DMA
    return pl.pallas_call(
        functools.partial(kernel, n),
        out_shape=jax.ShapeDtypeStruct((shard, WIDTH), BF16),
        in_specs=[pl.BlockSpec(memory_space=pltpu.SMEM), vmem, vmem, vmem],
        out_specs=vmem,
        scratch_shapes=[
            pltpu.VMEM((segs, SEG0, WIDTH), BF16),
            pltpu.VMEM((segs, SEG0, WIDTH), BF16),
            pltpu.VMEM((segs, SEG0, WIDTH), BF16),
            pltpu.VMEM((n, small, 2 * WIDTH), BF16),
            pltpu.VMEM((4, small, 2 * WIDTH), BF16),
            pltpu.VMEM((2, 2 * small, 2 * WIDTH), BF16),
            pltpu.VMEM((segs, LANES // 2, SEG0), BF16),
            pltpu.VMEM((HEADS, segs, SEG0, LANES), F32),
            pltpu.VMEM((HEADS, segs, SEG0 // 2, LANES), F32),
            pltpu.VMEM((segs, SEG0, WIDTH), BF16),
            dma((chips,)), dma((n,)), dma((2,)), dma((4,)), dma((1,)), dma((2,)),
            dma((chips,)), dma((1,)),
        ],
        compiler_params=pltpu.CompilerParams(
            collective_id=0, has_side_effects=True, vmem_limit_bytes=56 * 1024 * 1024
        ),
        cost_estimate=pl.CostEstimate(
            flops=256 * shard * HEADS * 1024, bytes_accessed=8 * shard * WIDTH,
            transcendentals=shard * HEADS * 1024,
        ),
    )(slide_length, query_tiles, key_tiles, value_tiles)


def solution(mesh):
    placed = P(("slide", "seq"), None)
    return jax.shard_map(
        functools.partial(per_device, mesh.shape["seq"]),
        mesh=mesh,
        in_specs=(placed, placed, placed, P("slide")),
        out_specs=placed,
        check_vma=False,
    )
```

```python
import functools
import math

import jax
import jax.numpy as jnp
from jax import lax
from jax.experimental import pallas as pl
from jax.experimental.pallas import tpu as pltpu
from jax.sharding import PartitionSpec as P

HEADS = 12
WIDTH = 768
SEG0 = 512
CLASSES = 16
PAIRS = HEADS // 2
RUN = SEG0 // CLASSES
LANES = 128
MESH = pl.DeviceIdType.MESH
BF16 = jnp.bfloat16
F32 = jnp.float32
EXP_SCALE = 0.125 * math.log2(math.e)
MASK = -1e9


def bitrev(c):
    return ((c & 1) << 3) + ((c & 2) << 1) + ((c & 4) >> 1) + ((c & 8) >> 3)


def home(j, side):
    return 8 * side + lax.rem(j, 2) * 4 + lax.rem(lax.div(j, 2), 2) * 2 + lax.div(j, 4)


def rows_at(start, size):
    return pl.ds(pl.multiple_of(start, RUN), size)


def pair_lanes(j, base=0):
    return pl.ds(pl.multiple_of(base + j * LANES, LANES), LANES)


def iota(shape, dim):
    return lax.broadcasted_iota(jnp.int32, shape, dim)


def staged(units):
    held = []
    for unit in units + [None, None]:
        if unit is not None:
            q, k, v, take = unit
            held.append((jnp.dot(q, k, preferred_element_type=F32), v, take))
        if len(held) > 2 or unit is None and held:
            scores, v, take = held.pop(0)
            columns = [scores[:, at:at + LANES] for at in range(0, scores.shape[1], LANES)]
            peak = jnp.max(functools.reduce(jnp.maximum, columns), axis=1, keepdims=True)
            weights = jnp.exp2((scores - peak) * EXP_SCALE).astype(BF16)
            take(jnp.dot(weights, v, preferred_element_type=F32), peak)


def merge(acc, peak, acc_b, peak_b):
    top = jnp.maximum(peak, peak_b)
    keep = jnp.exp2((peak - top) * EXP_SCALE)
    add = jnp.exp2((peak_b - top) * EXP_SCALE)
    return acc * keep + acc_b * add, top


def kernel(
    n, len_ref, q_ref, k_ref, v_ref, out_ref,
    qp, kp, vp, r16, r8, r4, bias0, acc_s, peak_s,
    send16, recv16, send8, recv8, send4, recv4, fwd16, fwd8,
):
    shard = q_ref.shape[0]
    segs = shard // SEG0
    chips = n // 2
    me = lax.axis_index("seq")
    chip, core = me // 2, me % 2
    sibling = chip * 2 + 1 - core
    mate_chip = chip + 1 - 2 * (chip % 2)
    mate = mate_chip * 2 + core
    length = len_ref[0]

    barrier = pltpu.get_barrier_semaphore()
    peers = [sibling] + [(chip + step) % chips * 2 + core for step in range(1, chips)]
    for peer in peers:
        pl.semaphore_signal(barrier, inc=1, device_id={"seq": peer}, device_id_type=MESH)

    half = SEG0 // 2
    sub = half // CLASSES
    new = iota((half, half), 0)
    old = iota((half, half), 1)
    shuffle = jnp.where(old == ((new & (sub - 1)) << 4) + bitrev(new >> 4), 1.0, 0.0).astype(BF16)

    def permute(src, dst):
        def column(step, _):
            lanes = pl.ds(pl.multiple_of(step * 256, 256), 256)
            for t in range(segs):
                for u in range(2):
                    rows = src[pl.ds(t * SEG0 + u * half, half), lanes]
                    moved = jnp.dot(shuffle, rows, preferred_element_type=F32).astype(BF16)
                    for i in range(CLASSES):
                        dst[t, pl.ds(i * RUN + u * sub, sub), lanes] = moved[i * sub:(i + 1) * sub]
            return 0
        lax.fori_loop(0, WIDTH // 256, column, 0)

    permute(k_ref, kp)
    permute(v_ref, vp)

    lane = iota((1, LANES), 1)
    even = jnp.where(lane < 64, 1.0, 0.0).astype(BF16)
    odd = jnp.where(lane < 64, 0.0, 1.0).astype(BF16)
    sides = ((even, odd), (odd, even))

    def gather(j, _):
        for src, base in ((kp, 0), (vp, WIDTH)):
            here = pair_lanes(j)
            there = pair_lanes(j, base)
            for t in range(segs):
                def mixed(turn, size):
                    e = src[t, rows_at(turn(home(j, 0)) * RUN, size), here]
                    o = src[t, rows_at(turn(home(j, 1)) * RUN, size), here]
                    return e * even + o * odd
                r16[me, pl.ds(t * RUN, RUN), there] = mixed(lambda c: c, RUN)
                r8[me % 4, pl.ds(t * RUN, RUN), there] = mixed(lambda c: c + 1 - 2 * lax.rem(c, 2), RUN)
                r4[me % 2, pl.ds(t * 2 * RUN, 2 * RUN), there] = mixed(lambda c: lax.div(c, 4) * 4 + 2 - lax.div(lax.rem(c, 4), 2) * 2, 2 * RUN)
        return 0

    lax.fori_loop(0, PAIRS, gather, 0)

    pl.semaphore_wait(barrier, chips)

    def copy(buf, slot, send, recv, peer):
        return pltpu.make_async_remote_copy(
            src_ref=buf.at[slot], dst_ref=buf.at[slot], send_sem=send, recv_sem=recv.at[slot],
            device_id={"seq": peer}, device_id_type=MESH,
        )

    first = []
    for step in range(chips - 1, 0, -1):
        first.append(copy(r16, me, send16.at[step], recv16, (chip + step) % chips * 2 + core))
    first.append(copy(r8, me % 4, send8.at[1], recv8, mate))
    first.append(copy(r16, me, send16.at[0], recv16, sibling))
    first.append(copy(r8, me % 4, send8.at[0], recv8, sibling))
    first.append(copy(r4, me % 2, send4.at[0], recv4, sibling))
    for c in first:
        c.start()

    permute(q_ref, qp)

    def bias_rows(place):
        fill = jnp.where(place < length, 0.0, MASK)
        return jnp.broadcast_to(fill, (LANES // 2, fill.shape[1])).astype(BF16)

    def one_head(kt, fill, side):
        mine = kt[side * 64:side * 64 + 64]
        return jnp.concatenate([fill, mine] if side else [mine, fill], axis=0)

    column = iota((1, SEG0), 1)
    for t in range(segs):
        place = me * shard + t * SEG0 + ((column & (RUN - 1)) << 4) + bitrev(column >> 5)
        bias0[t] = bias_rows(place)

    def near(j):
        here = pair_lanes(j)
        units = []
        kt = [jnp.transpose(kp[t, :, here]) for t in range(segs)]
        for side in range(2):
            mine, other = sides[side]
            h = 2 * j + side
            mid = pl.ds(side * half, half)
            low = pl.ds((1 - side) * half, half)

            full = [one_head(kt[t], bias0[t], side) for t in range(segs)]

            def keys(t, mid_rows):
                at = half if bool(side) == mid_rows else 0
                return full[t][:, at:at + half]

            def values(t, rows):
                return vp[t, rows, here] * mine + other

            def query(t, rows):
                return qp[t, rows, here] * mine + other

            def keep_low(t, h=h, low=low):
                def take(acc, peak):
                    acc_s[h, t, low, :] = acc
                return take

            def keep_mid(t, h=h, mid=mid):
                def take(acc, peak):
                    acc_s[h, t, mid, :] = acc
                    peak_s[h, t] = jnp.broadcast_to(peak, (half, LANES))
                return take

            k_all = jnp.concatenate(
                [keys(0, False), keys(0, True), keys(1, True), keys(1, False)], axis=1
            )
            low0, mid0, mid1, low1 = values(0, low), values(0, mid), values(1, mid), values(1, low)
            units += [
                (query(0, low), k_all[:, :2 * half], jnp.concatenate([low0, mid0], axis=0), keep_low(0)),
                (
                    query(0, mid), k_all[:, :3 * half],
                    jnp.concatenate([low0, mid0 + mid0, mid1], axis=0), keep_mid(0),
                ),
                (
                    query(1, mid), k_all[:, half:],
                    jnp.concatenate([mid0, mid1 + mid1, low1], axis=0), keep_mid(1),
                ),
                (query(1, low), k_all[:, 2 * half:], jnp.concatenate([mid1, low1], axis=0), keep_low(1)),
            ]
        return units

    def near_step(step, _):
        staged(near(2 * step) + near(2 * step + 1))
        return 0

    lax.fori_loop(0, PAIRS // 2, near_step, 0)

    second = []
    for step in range(1, chips):
        source = (chip + chips - step) % chips * 2 + core
        copy(r16, source, send16.at[step], recv16, sibling).wait_recv()
        c = copy(r16, source, fwd16.at[step], recv16, sibling)
        c.start()
        second.append(c)
    copy(r8, mate % 4, send8.at[1], recv8, sibling).wait_recv()
    c = copy(r8, mate % 4, fwd8.at[0], recv8, sibling)
    c.start()
    second.append(c)

    copy(r16, sibling, send16.at[0], recv16, sibling).wait_recv()
    copy(r8, sibling % 4, send8.at[0], recv8, sibling).wait_recv()
    copy(r4, sibling % 2, send4.at[0], recv4, sibling).wait_recv()
    def far(strides, j):
        here = pair_lanes(j)
        there = pair_lanes(j, WIDTH)

        def piece(buf, start, count, shift, keep, owner):
            size = buf.shape[1]
            bits = size.bit_length() - 1
            r = iota((1, count * size), 1)
            place = (
                (owner + (r >> bits)) * shard + ((r >> (bits - 1)) & 1) * SEG0
                + ((r & (RUN - 1)) << 4)
            )
            if size > segs * RUN:
                place = place + ((r >> 5) & 1) * 8
            k = buf[pl.ds(start, count), :, here].reshape(-1, LANES)
            v = buf[pl.ds(start, count), :, there].reshape(-1, LANES)
            return k, v, place, shift, keep

        def listed(pieces):
            k = jnp.concatenate([p[0] for p in pieces], axis=0)
            v = jnp.concatenate([p[1] for p in pieces], axis=0)
            return jnp.transpose(k), v, [p[2:] for p in pieces]

        two, four = me // 2 * 2, me // 4 * 4
        lists = []
        if 4 in strides:
            lists.append((4, listed((
                piece(r16, two, 2, 0, 16, two),
                piece(r8, two % 4, 2, 8, 16, two),
                piece(r4, 0, 2, 4, 8, two),
            ))))
        if 8 in strides:
            lists.append((8, listed((
                piece(r16, four, 4, 0, 16, four), piece(r8, 0, 4, 8, 16, four),
            ))))
        if 16 in strides:
            lists.append((16, listed((piece(r16, 0, n, 0, 16, 0),))))
        units = []
        for side in range(2):
            mine, other = sides[side]
            h = 2 * j + side
            for stride, (kt, values, places) in lists:
                size = SEG0 // stride
                group = CLASSES // stride
                start = lax.div(home(j, side), group) * size
                fill = jnp.concatenate(
                    [bias_rows(place + ((h + shift) & (keep - 1))) for place, shift, keep in places], axis=1
                )
                k, v = one_head(kt, fill, side), values * mine + other
                q = jnp.concatenate([qp[t, rows_at(start, size), here] for t in range(segs)], axis=0)

                def take(acc, peak, h=h, start=start, size=size, side=side):
                    rows = rows_at(start, size)
                    inner = rows_at(start - side * half, size)
                    for t in range(segs):
                        part = slice(t * size, (t + 1) * size)
                        acc_t, peak_t = merge(
                            acc_s[h, t, rows, :], peak_s[h, t, inner, :], acc[part], peak[part]
                        )
                        acc_s[h, t, rows, :] = acc_t
                        peak_s[h, t, inner, :] = peak_t

                units.append((q * mine + other, k, v, take))
        return units

    def finish(j):
        here = pair_lanes(j)
        wide = iota((SEG0, LANES), 1) < 64
        for t in range(segs):
            acc_e, acc_o = acc_s[2 * j, t], acc_s[2 * j + 1, t]
            total = pltpu.roll(jnp.where(wide, acc_o, acc_e), 64, 1)
            done = (jnp.where(wide, acc_e, acc_o) / total).astype(BF16)
            for u in range(2):
                for i in range(CLASSES):
                    at = i * RUN + u * sub
                    out_ref[pl.ds(t * SEG0 + u * half + i * sub, sub), here] = done[at:at + sub]

    def far_step(strides, step, _):
        staged(far(strides, 2 * step) + far(strides, 2 * step + 1))
        if 16 in strides:
            finish(2 * step)
            finish(2 * step + 1)
        return 0

    lax.fori_loop(0, PAIRS // 2, functools.partial(far_step, (4,)), 0)

    for step in range(1, chips):
        source = (chip + chips - step) % chips * 2 + 1 - core
        copy(r16, source, fwd16.at[step], recv16, sibling).wait_recv()
    far_mate = mate_chip * 2 + 1 - core
    copy(r8, far_mate % 4, fwd8.at[0], recv8, sibling).wait_recv()

    lax.fori_loop(0, PAIRS // 2, functools.partial(far_step, (8, 16)), 0)

    for c in first + second:
        c.wait_send()


def restore(len_ref, rows_ref, out_ref):
    half, width = rows_ref.shape
    sub = half // CLASSES
    new = iota((half, half), 0)
    old = iota((half, half), 1)
    back = jnp.where(new == ((old & (sub - 1)) << 4) + bitrev(old >> 4), 1.0, 0.0).astype(BF16)
    first = (lax.axis_index("seq") * pl.num_programs(0) + pl.program_id(0)) * half
    valid = first + iota((half, 1), 0) < len_ref[0]
    moved = jnp.dot(back, rows_ref[...], preferred_element_type=F32)
    out_ref[...] = jnp.where(valid, moved, 0.0).astype(BF16)


def per_device(n, query_tiles, key_tiles, value_tiles, slide_length):
    shard = query_tiles.shape[0]
    segs = shard // SEG0
    chips = n // 2
    small = segs * RUN
    vmem = pl.BlockSpec(memory_space=pltpu.VMEM)
    dma = pltpu.SemaphoreType.DMA
    shuffled = pl.pallas_call(
        functools.partial(kernel, n),
        out_shape=jax.ShapeDtypeStruct((shard, WIDTH), BF16),
        in_specs=[pl.BlockSpec(memory_space=pltpu.SMEM), vmem, vmem, vmem],
        out_specs=vmem,
        scratch_shapes=[
            pltpu.VMEM((segs, SEG0, WIDTH), BF16),
            pltpu.VMEM((segs, SEG0, WIDTH), BF16),
            pltpu.VMEM((segs, SEG0, WIDTH), BF16),
            pltpu.VMEM((n, small, 2 * WIDTH), BF16),
            pltpu.VMEM((4, small, 2 * WIDTH), BF16),
            pltpu.VMEM((2, 2 * small, 2 * WIDTH), BF16),
            pltpu.VMEM((segs, LANES // 2, SEG0), BF16),
            pltpu.VMEM((HEADS, segs, SEG0, LANES), F32),
            pltpu.VMEM((HEADS, segs, SEG0 // 2, LANES), F32),
            dma((chips,)), dma((n,)), dma((2,)), dma((4,)), dma((1,)), dma((2,)),
            dma((chips,)), dma((1,)),
        ],
        compiler_params=pltpu.CompilerParams(
            collective_id=0, has_side_effects=True, vmem_limit_bytes=56 * 1024 * 1024
        ),
        cost_estimate=pl.CostEstimate(
            flops=256 * shard * HEADS * 1024, bytes_accessed=8 * shard * WIDTH,
            transcendentals=shard * HEADS * 1024,
        ),
    )(slide_length, query_tiles, key_tiles, value_tiles)
    block = pl.BlockSpec((SEG0 // 2, WIDTH), lambda i: (i, 0))
    return pl.pallas_call(
        restore,
        grid=(shard // (SEG0 // 2),),
        out_shape=jax.ShapeDtypeStruct((shard, WIDTH), BF16),
        in_specs=[pl.BlockSpec(memory_space=pltpu.SMEM), block],
        out_specs=block,
    )(slide_length, shuffled)


def solution(mesh):
    placed = P(("slide", "seq"), None)
    return jax.shard_map(
        functools.partial(per_device, mesh.shape["seq"]),
        mesh=mesh,
        in_specs=(placed, placed, placed, P("slide")),
        out_specs=placed,
        check_vma=False,
    )
```

```python
import functools
import math

import jax
import jax.numpy as jnp
from jax import lax
from jax.experimental import pallas as pl
from jax.experimental.pallas import tpu as pltpu
from jax.sharding import PartitionSpec as P

HEADS = 12
WIDTH = 768
SEG0 = 512
CLASSES = 16
PAIRS = HEADS // 2
RUN = SEG0 // CLASSES
LANES = 128
MESH = pl.DeviceIdType.MESH
BF16 = jnp.bfloat16
F32 = jnp.float32
EXP_SCALE = 0.125 * math.log2(math.e)
MASK = -1e9


def bitrev(c):
    return ((c & 1) << 3) + ((c & 2) << 1) + ((c & 4) >> 1) + ((c & 8) >> 3)


def home(j, side):
    return 8 * side + lax.rem(j, 2) * 4 + lax.rem(lax.div(j, 2), 2) * 2 + lax.div(j, 4)


def rows_at(start, size):
    return pl.ds(pl.multiple_of(start, RUN), size)


def pair_lanes(j, base=0):
    return pl.ds(pl.multiple_of(base + j * LANES, LANES), LANES)


def iota(shape, dim):
    return lax.broadcasted_iota(jnp.int32, shape, dim)


def dot(a, b):
    return jnp.dot(a, b, preferred_element_type=F32)


def peak_of(*blocks):
    columns = [x[:, at:at + LANES] for x in blocks for at in range(0, x.shape[1], LANES)]
    return jnp.max(functools.reduce(jnp.maximum, columns), axis=1, keepdims=True)


def weigh(scores, peak):
    return jnp.exp2((scores - peak) * EXP_SCALE).astype(BF16)


def staged(units):
    held = None
    for unit in units + [None]:
        ahead = unit and (unit[0](), unit[1])
        if held is not None:
            held[1](*held[0])
        held = ahead


def merge(acc, peak, acc_b, peak_b):
    top = jnp.maximum(peak, peak_b)
    keep = jnp.exp2((peak - top) * EXP_SCALE)
    add = jnp.exp2((peak_b - top) * EXP_SCALE)
    return acc * keep + acc_b * add, top


def kernel(
    n, len_ref, q_ref, k_ref, v_ref, out_ref,
    qp, kp, vp, r16, r8, r4, bias0, acc_s, peak_s,
    send16, recv16, send8, recv8, send4, recv4, fwd16, fwd8,
):
    shard = q_ref.shape[0]
    segs = shard // SEG0
    chips = n // 2
    me = lax.axis_index("seq")
    chip, core = me // 2, me % 2
    sibling = chip * 2 + 1 - core
    mate_chip = chip + 1 - 2 * (chip % 2)
    mate = mate_chip * 2 + core
    length = len_ref[0]

    barrier = pltpu.get_barrier_semaphore()
    peers = [sibling] + [(chip + step) % chips * 2 + core for step in range(1, chips)]
    for peer in peers:
        pl.semaphore_signal(barrier, inc=1, device_id={"seq": peer}, device_id_type=MESH)

    half = SEG0 // 2
    sub = half // CLASSES
    new = iota((half, half), 0)
    old = iota((half, half), 1)
    shuffle = jnp.where(old == ((new & (sub - 1)) << 4) + bitrev(new >> 4), 1.0, 0.0).astype(BF16)

    def permute(src, dst):
        def column(step, _):
            lanes = pl.ds(pl.multiple_of(step * 256, 256), 256)
            for t in range(segs):
                for u in range(2):
                    rows = src[pl.ds(t * SEG0 + u * half, half), lanes]
                    moved = jnp.dot(shuffle, rows, preferred_element_type=F32).astype(BF16)
                    for i in range(CLASSES):
                        dst[t, pl.ds(i * RUN + u * sub, sub), lanes] = moved[i * sub:(i + 1) * sub]
            return 0
        lax.fori_loop(0, WIDTH // 256, column, 0)

    permute(k_ref, kp)
    permute(v_ref, vp)

    lane = iota((1, LANES), 1)
    even = jnp.where(lane < 64, 1.0, 0.0).astype(BF16)
    odd = jnp.where(lane < 64, 0.0, 1.0).astype(BF16)
    sides = ((even, odd), (odd, even))

    def gather(j, _):
        for src, base in ((kp, 0), (vp, WIDTH)):
            here = pair_lanes(j)
            there = pair_lanes(j, base)
            for t in range(segs):
                def mixed(turn, size):
                    e = src[t, rows_at(turn(home(j, 0)) * RUN, size), here]
                    o = src[t, rows_at(turn(home(j, 1)) * RUN, size), here]
                    return e * even + o * odd
                r16[me, pl.ds(t * RUN, RUN), there] = mixed(lambda c: c, RUN)
                r8[me % 4, pl.ds(t * RUN, RUN), there] = mixed(lambda c: c + 1 - 2 * lax.rem(c, 2), RUN)
                r4[me % 2, pl.ds(t * 2 * RUN, 2 * RUN), there] = mixed(lambda c: lax.div(c, 4) * 4 + 2 - lax.div(lax.rem(c, 4), 2) * 2, 2 * RUN)
        return 0

    lax.fori_loop(0, PAIRS, gather, 0)

    pl.semaphore_wait(barrier, chips)

    def copy(buf, slot, send, recv, peer):
        return pltpu.make_async_remote_copy(
            src_ref=buf.at[slot], dst_ref=buf.at[slot], send_sem=send, recv_sem=recv.at[slot],
            device_id={"seq": peer}, device_id_type=MESH,
        )

    first = []
    for step in range(chips - 1, 0, -1):
        first.append(copy(r16, me, send16.at[step], recv16, (chip + step) % chips * 2 + core))
    first.append(copy(r8, me % 4, send8.at[1], recv8, mate))
    first.append(copy(r16, me, send16.at[0], recv16, sibling))
    first.append(copy(r8, me % 4, send8.at[0], recv8, sibling))
    first.append(copy(r4, me % 2, send4.at[0], recv4, sibling))
    for c in first:
        c.start()

    permute(q_ref, qp)

    def bias_rows(place):
        fill = jnp.where(place < length, 0.0, MASK)
        return jnp.broadcast_to(fill, (LANES // 2, fill.shape[1])).astype(BF16)

    wide = iota((1, LANES), 1) < LANES // 2

    def query(q, side):
        mine = sides[side][0]
        return jnp.concatenate([q * mine, jnp.zeros_like(q) + mine], axis=1)

    def with_ones(v):
        return jnp.concatenate([v, jnp.ones_like(v)], axis=1)

    def own_half(acc, side):
        sums, totals = acc[:, :LANES], acc[:, LANES:]
        return jnp.where(wide, totals, sums) if side else jnp.where(wide, sums, totals)

    column = iota((1, SEG0), 1)
    for t in range(segs):
        place = me * shard + t * SEG0 + ((column & (RUN - 1)) << 4) + bitrev(column >> 5)
        bias0[t] = bias_rows(place)

    def near(j):
        here = pair_lanes(j)
        keys = [
            jnp.concatenate([jnp.transpose(kp[t, :, here]), bias0[t], bias0[t]], axis=0)
            for t in range(segs)
        ]
        values = [with_ones(vp[t, :, here]) for t in range(segs)]

        def unit(t):
            far_t = 1 - t

            def start():
                q = [query(qp[t, :, here], side) for side in range(2)]
                own = dot(jnp.concatenate(q, axis=0), keys[t])
                cross = []
                for side in range(2):
                    mid = slice(side * half, side * half + half)
                    cross.append(dot(q[side][mid], keys[far_t][:, mid]))
                return own, cross

            def take(own, cross):
                rows = []
                extra = []
                for side in range(2):
                    h = 2 * j + side
                    for block in range(2):
                        at = (2 * side + block) * half
                        scores = own[at:at + half]
                        if block != side:
                            rows.append(weigh(scores, peak_of(scores)))
                            continue
                        peak = peak_of(scores, cross[side])
                        weights = weigh(scores, peak)
                        left, right = weights[:, :half], weights[:, half:]
                        if side:
                            right = right + right
                        else:
                            left = left + left
                        rows.append(jnp.concatenate([left, right], axis=1))
                        mid = slice(side * half, side * half + half)
                        extra.append(dot(weigh(cross[side], peak), values[far_t][mid]))
                        peak_s[h, t] = jnp.broadcast_to(peak, (half, LANES))
                acc = dot(jnp.concatenate(rows, axis=0), values[t])
                for side in range(2):
                    for block in range(2):
                        at = (2 * side + block) * half
                        part = acc[at:at + half]
                        if block == side:
                            part = part + extra[side]
                        acc_s[2 * j + side, t, pl.ds(block * half, half), :] = own_half(part, side)

            return start, take

        return [unit(t) for t in range(segs)]

    def near_step(step, _):
        staged(near(2 * step) + near(2 * step + 1))
        return 0

    lax.fori_loop(0, PAIRS // 2, near_step, 0)

    second = []
    for step in range(1, chips):
        source = (chip + chips - step) % chips * 2 + core
        copy(r16, source, send16.at[step], recv16, sibling).wait_recv()
        c = copy(r16, source, fwd16.at[step], recv16, sibling)
        c.start()
        second.append(c)
    copy(r8, mate % 4, send8.at[1], recv8, sibling).wait_recv()
    c = copy(r8, mate % 4, fwd8.at[0], recv8, sibling)
    c.start()
    second.append(c)

    copy(r16, sibling, send16.at[0], recv16, sibling).wait_recv()
    copy(r8, sibling % 4, send8.at[0], recv8, sibling).wait_recv()
    copy(r4, sibling % 2, send4.at[0], recv4, sibling).wait_recv()
    def far(strides, j):
        here = pair_lanes(j)
        there = pair_lanes(j, WIDTH)

        def piece(buf, start, count, shift, keep, owner):
            size = buf.shape[1]
            bits = size.bit_length() - 1
            r = iota((1, count * size), 1)
            place = (
                (owner + (r >> bits)) * shard + ((r >> (bits - 1)) & 1) * SEG0
                + ((r & (RUN - 1)) << 4)
            )
            if size > segs * RUN:
                place = place + ((r >> 5) & 1) * 8
            k = buf[pl.ds(start, count), :, here].reshape(-1, LANES)
            v = buf[pl.ds(start, count), :, there].reshape(-1, LANES)
            return k, v, place, shift, keep

        def listed(pieces):
            k = jnp.concatenate([p[0] for p in pieces], axis=0)
            v = jnp.concatenate([p[1] for p in pieces], axis=0)
            return jnp.transpose(k), v, [p[2:] for p in pieces]

        two, four = me // 2 * 2, me // 4 * 4
        lists = []
        if 4 in strides:
            lists.append((4, listed((
                piece(r16, two, 2, 0, 16, two),
                piece(r8, two % 4, 2, 8, 16, two),
                piece(r4, 0, 2, 4, 8, two),
            ))))
        if 8 in strides:
            lists.append((8, listed((
                piece(r16, four, 4, 0, 16, four), piece(r8, 0, 4, 8, 16, four),
            ))))
        if 16 in strides:
            lists.append((16, listed((piece(r16, 0, n, 0, 16, 0),))))
        def unit(stride, kt, v, places):
            size = SEG0 // stride
            group = CLASSES // stride
            count = segs * size
            starts = [lax.div(home(j, side), group) * size for side in range(2)]

            def start():
                fills = [
                    jnp.concatenate(
                        [
                            bias_rows(place + ((2 * j + side + shift) & (keep - 1)))
                            for place, shift, keep in places
                        ],
                        axis=1,
                    )
                    for side in range(2)
                ]
                q = [
                    query(qp[t, rows_at(starts[side], size), here], side)
                    for side in range(2) for t in range(segs)
                ]
                return (dot(jnp.concatenate(q, axis=0), jnp.concatenate([kt] + fills, axis=0)),)

            def take(scores):
                peak = peak_of(scores)
                acc = dot(weigh(scores, peak), with_ones(v))
                for side in range(2):
                    h = 2 * j + side
                    rows = rows_at(starts[side], size)
                    inner = rows_at(starts[side] - side * half, size)
                    for t in range(segs):
                        at = side * count + t * size
                        acc_t, peak_t = merge(
                            acc_s[h, t, rows, :], peak_s[h, t, inner, :],
                            own_half(acc[at:at + size], side), peak[at:at + size],
                        )
                        acc_s[h, t, rows, :] = acc_t
                        peak_s[h, t, inner, :] = peak_t

            return start, take

        return [unit(stride, *rest) for stride, rest in lists]

    def finish(j):
        here = pair_lanes(j)
        for t in range(segs):
            acc_e, acc_o = acc_s[2 * j, t], acc_s[2 * j + 1, t]
            total = pltpu.roll(jnp.where(wide, acc_o, acc_e), 64, 1)
            done = (jnp.where(wide, acc_e, acc_o) / total).astype(BF16)
            for u in range(2):
                for i in range(CLASSES):
                    at = i * RUN + u * sub
                    out_ref[pl.ds(t * SEG0 + u * half + i * sub, sub), here] = done[at:at + sub]

    def far_step(strides, step, _):
        staged(far(strides, 2 * step) + far(strides, 2 * step + 1))
        if 16 in strides:
            finish(2 * step)
            finish(2 * step + 1)
        return 0

    lax.fori_loop(0, PAIRS // 2, functools.partial(far_step, (4,)), 0)

    for step in range(1, chips):
        source = (chip + chips - step) % chips * 2 + 1 - core
        copy(r16, source, fwd16.at[step], recv16, sibling).wait_recv()
    far_mate = mate_chip * 2 + 1 - core
    copy(r8, far_mate % 4, fwd8.at[0], recv8, sibling).wait_recv()

    lax.fori_loop(0, PAIRS // 2, functools.partial(far_step, (8, 16)), 0)

    for c in first + second:
        c.wait_send()


def restore(len_ref, rows_ref, out_ref):
    half, width = rows_ref.shape
    sub = half // CLASSES
    new = iota((half, half), 0)
    old = iota((half, half), 1)
    back = jnp.where(new == ((old & (sub - 1)) << 4) + bitrev(old >> 4), 1.0, 0.0).astype(BF16)
    first = (lax.axis_index("seq") * pl.num_programs(0) + pl.program_id(0)) * half
    valid = first + iota((half, 1), 0) < len_ref[0]
    moved = jnp.dot(back, rows_ref[...], preferred_element_type=F32)
    out_ref[...] = jnp.where(valid, moved, 0.0).astype(BF16)


def per_device(n, query_tiles, key_tiles, value_tiles, slide_length):
    shard = query_tiles.shape[0]
    segs = shard // SEG0
    chips = n // 2
    small = segs * RUN
    vmem = pl.BlockSpec(memory_space=pltpu.VMEM)
    dma = pltpu.SemaphoreType.DMA
    shuffled = pl.pallas_call(
        functools.partial(kernel, n),
        out_shape=jax.ShapeDtypeStruct((shard, WIDTH), BF16),
        in_specs=[pl.BlockSpec(memory_space=pltpu.SMEM), vmem, vmem, vmem],
        out_specs=vmem,
        scratch_shapes=[
            pltpu.VMEM((segs, SEG0, WIDTH), BF16),
            pltpu.VMEM((segs, SEG0, WIDTH), BF16),
            pltpu.VMEM((segs, SEG0, WIDTH), BF16),
            pltpu.VMEM((n, small, 2 * WIDTH), BF16),
            pltpu.VMEM((4, small, 2 * WIDTH), BF16),
            pltpu.VMEM((2, 2 * small, 2 * WIDTH), BF16),
            pltpu.VMEM((segs, LANES // 2, SEG0), BF16),
            pltpu.VMEM((HEADS, segs, SEG0, LANES), F32),
            pltpu.VMEM((HEADS, segs, SEG0 // 2, LANES), F32),
            dma((chips,)), dma((n,)), dma((2,)), dma((4,)), dma((1,)), dma((2,)),
            dma((chips,)), dma((1,)),
        ],
        compiler_params=pltpu.CompilerParams(
            collective_id=0, has_side_effects=True, vmem_limit_bytes=56 * 1024 * 1024
        ),
        cost_estimate=pl.CostEstimate(
            flops=256 * shard * HEADS * 1024, bytes_accessed=8 * shard * WIDTH,
            transcendentals=shard * HEADS * 1024,
        ),
    )(slide_length, query_tiles, key_tiles, value_tiles)
    block = pl.BlockSpec((SEG0 // 2, WIDTH), lambda i: (i, 0))
    return pl.pallas_call(
        restore,
        grid=(shard // (SEG0 // 2),),
        out_shape=jax.ShapeDtypeStruct((shard, WIDTH), BF16),
        in_specs=[pl.BlockSpec(memory_space=pltpu.SMEM), block],
        out_specs=block,
    )(slide_length, shuffled)


def solution(mesh):
    placed = P(("slide", "seq"), None)
    return jax.shard_map(
        functools.partial(per_device, mesh.shape["seq"]),
        mesh=mesh,
        in_specs=(placed, placed, placed, P("slide")),
        out_specs=placed,
        check_vma=False,
    )
```

```python
import functools
import math

import jax
import jax.numpy as jnp
from jax import lax
from jax.experimental import pallas as pl
from jax.experimental.pallas import tpu as pltpu
from jax.sharding import PartitionSpec as P

HEADS = 12
WIDTH = 768
SEG0 = 512
CLASSES = 16
PAIRS = HEADS // 2
RUN = SEG0 // CLASSES
LANES = 128
MESH = pl.DeviceIdType.MESH
BF16 = jnp.bfloat16
F32 = jnp.float32
EXP_SCALE = 0.125 * math.log2(math.e)
MASK = -1e9


def bitrev(c):
    return ((c & 1) << 3) + ((c & 2) << 1) + ((c & 4) >> 1) + ((c & 8) >> 3)


def home(j, side):
    return 8 * side + lax.rem(j, 2) * 4 + lax.rem(lax.div(j, 2), 2) * 2 + lax.div(j, 4)


def rows_at(start, size):
    return pl.ds(pl.multiple_of(start, RUN), size)


def pair_lanes(j, base=0):
    return pl.ds(pl.multiple_of(base + j * LANES, LANES), LANES)


def iota(shape, dim):
    return lax.broadcasted_iota(jnp.int32, shape, dim)


def dot(a, b):
    return jnp.dot(a, b, preferred_element_type=F32)


def peak_of(*blocks):
    columns = [x[:, at:at + LANES] for x in blocks for at in range(0, x.shape[1], LANES)]
    return jnp.max(functools.reduce(jnp.maximum, columns), axis=1, keepdims=True)


def weigh(scores, peak):
    return jnp.exp2((scores - peak) * EXP_SCALE).astype(BF16)


def staged(units):
    held = None
    for unit in units + [None]:
        ahead = unit and (unit[0](), unit[1])
        if held is not None:
            held[1](*held[0])
        held = ahead


def merge(acc, peak, acc_b, peak_b):
    top = jnp.maximum(peak, peak_b)
    keep = jnp.exp2((peak - top) * EXP_SCALE)
    add = jnp.exp2((peak_b - top) * EXP_SCALE)
    return acc * keep + acc_b * add, top


def kernel(
    n, len_ref, q_hbm, k_hbm, v_hbm, out_ref,
    q_ref, k_ref, v_ref, load, qp, kp, vp, r16, r8, r4, bias0, acc_s, peak_s,
    send16, recv16, send8, recv8, send4, recv4, fwd16, fwd8,
):
    loads = [
        pltpu.make_async_copy(src, dst, load.at[i])
        for i, (src, dst) in enumerate(((k_hbm, k_ref), (v_hbm, v_ref), (q_hbm, q_ref)))
    ]
    for c in loads:
        c.start()
    shard = q_ref.shape[0]
    segs = shard // SEG0
    chips = n // 2
    me = lax.axis_index("seq")
    chip, core = me // 2, me % 2
    sibling = chip * 2 + 1 - core
    mate_chip = chip + 1 - 2 * (chip % 2)
    mate = mate_chip * 2 + core
    length = len_ref[0]

    barrier = pltpu.get_barrier_semaphore()
    peers = [sibling] + [(chip + step) % chips * 2 + core for step in range(1, chips)]
    for peer in peers:
        pl.semaphore_signal(barrier, inc=1, device_id={"seq": peer}, device_id_type=MESH)

    half = SEG0 // 2
    sub = half // CLASSES
    new = iota((half, half), 0)
    old = iota((half, half), 1)
    shuffle = jnp.where(old == ((new & (sub - 1)) << 4) + bitrev(new >> 4), 1.0, 0.0).astype(BF16)

    def permute(src, dst):
        def column(step, _):
            lanes = pl.ds(pl.multiple_of(step * 256, 256), 256)
            for t in range(segs):
                for u in range(2):
                    rows = src[pl.ds(t * SEG0 + u * half, half), lanes]
                    moved = jnp.dot(shuffle, rows, preferred_element_type=F32).astype(BF16)
                    for i in range(CLASSES):
                        dst[t, pl.ds(i * RUN + u * sub, sub), lanes] = moved[i * sub:(i + 1) * sub]
            return 0
        lax.fori_loop(0, WIDTH // 256, column, 0)

    loads[0].wait()
    permute(k_ref, kp)
    loads[1].wait()
    permute(v_ref, vp)

    lane = iota((1, LANES), 1)
    even = jnp.where(lane < 64, 1.0, 0.0).astype(BF16)
    odd = jnp.where(lane < 64, 0.0, 1.0).astype(BF16)
    sides = ((even, odd), (odd, even))

    def gather(j, _):
        for src, base in ((kp, 0), (vp, WIDTH)):
            here = pair_lanes(j)
            there = pair_lanes(j, base)
            for t in range(segs):
                def mixed(turn, size):
                    e = src[t, rows_at(turn(home(j, 0)) * RUN, size), here]
                    o = src[t, rows_at(turn(home(j, 1)) * RUN, size), here]
                    return e * even + o * odd
                r16[me, pl.ds(t * RUN, RUN), there] = mixed(lambda c: c, RUN)
                r8[me % 4, pl.ds(t * RUN, RUN), there] = mixed(lambda c: c + 1 - 2 * lax.rem(c, 2), RUN)
                r4[me % 2, pl.ds(t * 2 * RUN, 2 * RUN), there] = mixed(lambda c: lax.div(c, 4) * 4 + 2 - lax.div(lax.rem(c, 4), 2) * 2, 2 * RUN)
        return 0

    lax.fori_loop(0, PAIRS, gather, 0)

    pl.semaphore_wait(barrier, chips)

    def copy(buf, slot, send, recv, peer):
        return pltpu.make_async_remote_copy(
            src_ref=buf.at[slot], dst_ref=buf.at[slot], send_sem=send, recv_sem=recv.at[slot],
            device_id={"seq": peer}, device_id_type=MESH,
        )

    turn = chip % 2
    first = [
        copy(r8, me % 4, send8.at[1], recv8, mate),
        copy(r16, me, send16.at[chips], recv16, mate),
        copy(r16, me, send16.at[0], recv16, sibling),
        copy(r8, me % 4, send8.at[0], recv8, sibling),
        copy(r4, me % 2, send4.at[0], recv4, sibling),
    ]
    others = [(mate_chip + (1 - 2 * turn) * step + chips) % chips for step in range(1, chips - 1)]
    for step, other_chip in enumerate(others):
        first.append(copy(r16, me, send16.at[step + 1], recv16, other_chip * 2 + core))
    for c in first:
        c.start()

    loads[2].wait()
    permute(q_ref, qp)

    def bias_rows(place):
        fill = jnp.where(place < length, 0.0, MASK)
        return jnp.broadcast_to(fill, (LANES // 2, fill.shape[1])).astype(BF16)

    wide = iota((1, LANES), 1) < LANES // 2

    def query(q, side):
        mine = sides[side][0]
        return jnp.concatenate([q * mine, jnp.zeros_like(q) + mine], axis=1)

    def with_ones(v):
        return jnp.concatenate([v, jnp.ones_like(v)], axis=1)

    def own_half(acc, side):
        sums, totals = acc[:, :LANES], acc[:, LANES:]
        return jnp.where(wide, totals, sums) if side else jnp.where(wide, sums, totals)

    column = iota((1, SEG0), 1)
    for t in range(segs):
        place = me * shard + t * SEG0 + ((column & (RUN - 1)) << 4) + bitrev(column >> 5)
        bias0[t] = bias_rows(place)

    def near(j):
        here = pair_lanes(j)
        keys = [
            jnp.concatenate([jnp.transpose(kp[t, :, here]), bias0[t], bias0[t]], axis=0)
            for t in range(segs)
        ]
        values = [with_ones(vp[t, :, here]) for t in range(segs)]

        def unit(t):
            far_t = 1 - t

            def start():
                q = [query(qp[t, :, here], side) for side in range(2)]
                own = dot(jnp.concatenate(q, axis=0), keys[t])
                cross = []
                for side in range(2):
                    mid = slice(side * half, side * half + half)
                    cross.append(dot(q[side][mid], keys[far_t][:, mid]))
                return own, cross

            def take(own, cross):
                rows = []
                extra = []
                for side in range(2):
                    h = 2 * j + side
                    for block in range(2):
                        at = (2 * side + block) * half
                        scores = own[at:at + half]
                        if block != side:
                            rows.append(weigh(scores, peak_of(scores)))
                            continue
                        peak = peak_of(scores, cross[side])
                        weights = weigh(scores, peak)
                        left, right = weights[:, :half], weights[:, half:]
                        if side:
                            right = right + right
                        else:
                            left = left + left
                        rows.append(jnp.concatenate([left, right], axis=1))
                        mid = slice(side * half, side * half + half)
                        extra.append(dot(weigh(cross[side], peak), values[far_t][mid]))
                        peak_s[h, t] = jnp.broadcast_to(peak, (half, LANES))
                acc = dot(jnp.concatenate(rows, axis=0), values[t])
                for side in range(2):
                    for block in range(2):
                        at = (2 * side + block) * half
                        part = acc[at:at + half]
                        if block == side:
                            part = part + extra[side]
                        acc_s[2 * j + side, t, pl.ds(block * half, half), :] = own_half(part, side)

            return start, take

        return [unit(t) for t in range(segs)]

    def near_step(step, _):
        staged(near(2 * step) + near(2 * step + 1))
        return 0

    lax.fori_loop(0, PAIRS // 2, near_step, 0)

    copy(r16, sibling, send16.at[0], recv16, sibling).wait_recv()
    copy(r8, sibling % 4, send8.at[0], recv8, sibling).wait_recv()
    copy(r4, sibling % 2, send4.at[0], recv4, sibling).wait_recv()
    def far(strides, j):
        here = pair_lanes(j)
        there = pair_lanes(j, WIDTH)

        def piece(buf, start, count, shift, keep, owner):
            size = buf.shape[1]
            bits = size.bit_length() - 1
            r = iota((1, count * size), 1)
            place = (
                (owner + (r >> bits)) * shard + ((r >> (bits - 1)) & 1) * SEG0
                + ((r & (RUN - 1)) << 4)
            )
            if size > segs * RUN:
                place = place + ((r >> 5) & 1) * 8
            k = buf[pl.ds(start, count), :, here].reshape(-1, LANES)
            v = buf[pl.ds(start, count), :, there].reshape(-1, LANES)
            return k, v, place, shift, keep

        def listed(pieces):
            k = jnp.concatenate([p[0] for p in pieces], axis=0)
            v = jnp.concatenate([p[1] for p in pieces], axis=0)
            return jnp.transpose(k), v, [p[2:] for p in pieces]

        two, four = me // 2 * 2, me // 4 * 4
        lists = []
        if 4 in strides:
            lists.append((4, listed((
                piece(r16, two, 2, 0, 16, two),
                piece(r8, two % 4, 2, 8, 16, two),
                piece(r4, 0, 2, 4, 8, two),
            ))))
        if 8 in strides:
            lists.append((8, listed((
                piece(r16, four, 4, 0, 16, four), piece(r8, 0, 4, 8, 16, four),
            ))))
        if 16 in strides:
            lists.append((16, listed((piece(r16, 0, n, 0, 16, 0),))))
        def unit(stride, kt, v, places):
            size = SEG0 // stride
            group = CLASSES // stride
            count = segs * size
            starts = [lax.div(home(j, side), group) * size for side in range(2)]

            def start():
                fills = [
                    jnp.concatenate(
                        [
                            bias_rows(place + ((2 * j + side + shift) & (keep - 1)))
                            for place, shift, keep in places
                        ],
                        axis=1,
                    )
                    for side in range(2)
                ]
                q = [
                    query(qp[t, rows_at(starts[side], size), here], side)
                    for side in range(2) for t in range(segs)
                ]
                return (dot(jnp.concatenate(q, axis=0), jnp.concatenate([kt] + fills, axis=0)),)

            def take(scores):
                peak = peak_of(scores)
                acc = dot(weigh(scores, peak), with_ones(v))
                for side in range(2):
                    h = 2 * j + side
                    rows = rows_at(starts[side], size)
                    inner = rows_at(starts[side] - side * half, size)
                    for t in range(segs):
                        at = side * count + t * size
                        acc_t, peak_t = merge(
                            acc_s[h, t, rows, :], peak_s[h, t, inner, :],
                            own_half(acc[at:at + size], side), peak[at:at + size],
                        )
                        acc_s[h, t, rows, :] = acc_t
                        peak_s[h, t, inner, :] = peak_t

            return start, take

        return [unit(stride, *rest) for stride, rest in lists]

    def finish(j):
        here = pair_lanes(j)
        for t in range(segs):
            acc_e, acc_o = acc_s[2 * j, t], acc_s[2 * j + 1, t]
            total = pltpu.roll(jnp.where(wide, acc_o, acc_e), 64, 1)
            done = (jnp.where(wide, acc_e, acc_o) / total).astype(BF16)
            for u in range(2):
                for i in range(CLASSES):
                    at = i * RUN + u * sub
                    out_ref[pl.ds(t * SEG0 + u * half + i * sub, sub), here] = done[at:at + sub]

    def far_step(strides, step, _):
        staged(far(strides, 2 * step) + far(strides, 2 * step + 1))
        if 16 in strides:
            finish(2 * step)
            finish(2 * step + 1)
        return 0

    lax.fori_loop(0, PAIRS // 2, functools.partial(far_step, (4,)), 0)

    def forward(buf, slot, arrived, sent, recv):
        copy(buf, slot, arrived, recv, sibling).wait_recv()
        c = copy(buf, slot, sent, recv, sibling)
        c.start()
        return c

    second = [
        forward(r8, mate % 4, send8.at[1], fwd8.at[0], recv8),
        forward(r16, mate, send16.at[chips], fwd16.at[0], recv16),
    ]
    for step, other_chip in enumerate(others):
        second.append(
            forward(r16, other_chip * 2 + core, send16.at[step + 1], fwd16.at[step + 1], recv16)
        )

    far_mate = mate_chip * 2 + 1 - core
    copy(r8, far_mate % 4, fwd8.at[0], recv8, sibling).wait_recv()
    copy(r16, far_mate, fwd16.at[0], recv16, sibling).wait_recv()
    lax.fori_loop(0, PAIRS // 2, functools.partial(far_step, (8,)), 0)

    for step, other_chip in enumerate(others):
        source = other_chip * 2 + 1 - core
        copy(r16, source, fwd16.at[step + 1], recv16, sibling).wait_recv()
    lax.fori_loop(0, PAIRS // 2, functools.partial(far_step, (16,)), 0)

    for c in first + second:
        c.wait_send()


def restore(len_ref, rows_ref, out_ref):
    half, width = rows_ref.shape
    sub = half // CLASSES
    new = iota((half, half), 0)
    old = iota((half, half), 1)
    back = jnp.where(new == ((old & (sub - 1)) << 4) + bitrev(old >> 4), 1.0, 0.0).astype(BF16)
    first = (lax.axis_index("seq") * pl.num_programs(0) + pl.program_id(0)) * half
    valid = first + iota((half, 1), 0) < len_ref[0]
    moved = jnp.dot(back, rows_ref[...], preferred_element_type=F32)
    out_ref[...] = jnp.where(valid, moved, 0.0).astype(BF16)


def per_device(n, query_tiles, key_tiles, value_tiles, slide_length):
    shard = query_tiles.shape[0]
    segs = shard // SEG0
    chips = n // 2
    small = segs * RUN
    vmem = pl.BlockSpec(memory_space=pltpu.VMEM)
    dma = pltpu.SemaphoreType.DMA
    shuffled = pl.pallas_call(
        functools.partial(kernel, n),
        out_shape=pltpu.VMEM((shard, WIDTH), BF16),
        in_specs=[pl.BlockSpec(memory_space=pltpu.SMEM)] + [pl.BlockSpec(memory_space=pl.ANY)] * 3,
        out_specs=vmem,
        scratch_shapes=[
            pltpu.VMEM((shard, WIDTH), BF16),
            pltpu.VMEM((shard, WIDTH), BF16),
            pltpu.VMEM((shard, WIDTH), BF16),
            dma((3,)),
            pltpu.VMEM((segs, SEG0, WIDTH), BF16),
            pltpu.VMEM((segs, SEG0, WIDTH), BF16),
            pltpu.VMEM((segs, SEG0, WIDTH), BF16),
            pltpu.VMEM((n, small, 2 * WIDTH), BF16),
            pltpu.VMEM((4, small, 2 * WIDTH), BF16),
            pltpu.VMEM((2, 2 * small, 2 * WIDTH), BF16),
            pltpu.VMEM((segs, LANES // 2, SEG0), BF16),
            pltpu.VMEM((HEADS, segs, SEG0, LANES), F32),
            pltpu.VMEM((HEADS, segs, SEG0 // 2, LANES), F32),
            dma((chips + 1,)), dma((n,)), dma((2,)), dma((4,)), dma((1,)), dma((2,)),
            dma((chips,)), dma((1,)),
        ],
        compiler_params=pltpu.CompilerParams(
            collective_id=0, has_side_effects=True, vmem_limit_bytes=56 * 1024 * 1024
        ),
        cost_estimate=pl.CostEstimate(
            flops=256 * shard * HEADS * 1024, bytes_accessed=8 * shard * WIDTH,
            transcendentals=shard * HEADS * 1024,
        ),
    )(slide_length, query_tiles, key_tiles, value_tiles)
    block = pl.BlockSpec((SEG0 // 2, WIDTH), lambda i: (i, 0))
    return pl.pallas_call(
        restore,
        grid=(shard // (SEG0 // 2),),
        out_shape=jax.ShapeDtypeStruct((shard, WIDTH), BF16),
        in_specs=[pl.BlockSpec(memory_space=pltpu.SMEM), block],
        out_specs=block,
    )(slide_length, shuffled)


def solution(mesh):
    placed = P(("slide", "seq"), None)
    return jax.shard_map(
        functools.partial(per_device, mesh.shape["seq"]),
        mesh=mesh,
        in_specs=(placed, placed, placed, P("slide")),
        out_specs=placed,
        check_vma=False,
    )
```

```python
import functools
import math

import jax
import jax.numpy as jnp
from jax import lax
from jax.experimental import pallas as pl
from jax.experimental.pallas import tpu as pltpu
from jax.sharding import PartitionSpec as P

HEADS = 12
WIDTH = 768
SEG0 = 512
CLASSES = 16
PAIRS = HEADS // 2
RUN = SEG0 // CLASSES
LANES = 128
MESH = pl.DeviceIdType.MESH
BF16 = jnp.bfloat16
F32 = jnp.float32
EXP_SCALE = 0.125 * math.log2(math.e)
MASK = -1e9


def bitrev(c):
    return ((c & 1) << 3) + ((c & 2) << 1) + ((c & 4) >> 1) + ((c & 8) >> 3)


def home(j, side):
    return 8 * side + lax.rem(j, 2) * 4 + lax.rem(lax.div(j, 2), 2) * 2 + lax.div(j, 4)


def rows_at(start, size):
    return pl.ds(pl.multiple_of(start, RUN), size)


def pair_lanes(j, base=0):
    return pl.ds(pl.multiple_of(base + j * LANES, LANES), LANES)


def iota(shape, dim):
    return lax.broadcasted_iota(jnp.int32, shape, dim)


def dot(a, b):
    return jnp.dot(a, b, preferred_element_type=F32)


def peak_of(*blocks):
    columns = [x[:, at:at + LANES] for x in blocks for at in range(0, x.shape[1], LANES)]
    return jnp.max(functools.reduce(jnp.maximum, columns), axis=1, keepdims=True)


def weigh(scores, peak):
    return jnp.exp2((scores - peak) * EXP_SCALE).astype(BF16)


def staged(units):
    held = None
    for unit in units + [None]:
        ahead = unit and (unit[0](), unit[1])
        if held is not None:
            held[1](*held[0])
        held = ahead


def merge(acc, peak, acc_b, peak_b):
    top = jnp.maximum(peak, peak_b)
    keep = jnp.exp2((peak - top) * EXP_SCALE)
    add = jnp.exp2((peak_b - top) * EXP_SCALE)
    return acc * keep + acc_b * add, top


def kernel(
    n, len_ref, q_hbm, k_hbm, v_hbm, out_ref,
    q_ref, k_ref, v_ref, load, qp, kp, vp, r16, r8, r4, bias0, acc_s, peak_s,
    send16, recv16, send8, recv8, send4, recv4, fwd16, fwd8,
):
    loads = [
        pltpu.make_async_copy(src, dst, load.at[i])
        for i, (src, dst) in enumerate(((k_hbm, k_ref), (v_hbm, v_ref), (q_hbm, q_ref)))
    ]
    for c in loads:
        c.start()
    shard = q_ref.shape[0]
    segs = shard // SEG0
    chips = n // 2
    me = lax.axis_index("seq")
    chip, core = me // 2, me % 2
    sibling = chip * 2 + 1 - core
    mate_chip = chip + 1 - 2 * (chip % 2)
    mate = mate_chip * 2 + core
    length = len_ref[0]

    barrier = pltpu.get_barrier_semaphore()
    peers = [sibling] + [(chip + step) % chips * 2 + core for step in range(1, chips)]
    for peer in peers:
        pl.semaphore_signal(barrier, inc=1, device_id={"seq": peer}, device_id_type=MESH)

    half = SEG0 // 2
    sub = half // CLASSES
    new = iota((half, half), 0)
    old = iota((half, half), 1)
    shuffle = jnp.where(old == ((new & (sub - 1)) << 4) + bitrev(new >> 4), 1.0, 0.0).astype(BF16)

    def permute(src, dst):
        def column(step, _):
            lanes = pl.ds(pl.multiple_of(step * 256, 256), 256)
            for t in range(segs):
                for u in range(2):
                    rows = src[pl.ds(t * SEG0 + u * half, half), lanes]
                    moved = jnp.dot(shuffle, rows, preferred_element_type=F32).astype(BF16)
                    for i in range(CLASSES):
                        dst[t, pl.ds(i * RUN + u * sub, sub), lanes] = moved[i * sub:(i + 1) * sub]
            return 0
        lax.fori_loop(0, WIDTH // 256, column, 0)

    loads[0].wait()
    permute(k_ref, kp)
    loads[1].wait()
    permute(v_ref, vp)

    lane = iota((1, LANES), 1)
    even = jnp.where(lane < 64, 1.0, 0.0).astype(BF16)
    odd = jnp.where(lane < 64, 0.0, 1.0).astype(BF16)
    sides = ((even, odd), (odd, even))

    def gather(j, _):
        for src, base in ((kp, 0), (vp, WIDTH)):
            here = pair_lanes(j)
            there = pair_lanes(j, base)
            for t in range(segs):
                def mixed(turn, size):
                    e = src[t, rows_at(turn(home(j, 0)) * RUN, size), here]
                    o = src[t, rows_at(turn(home(j, 1)) * RUN, size), here]
                    return e * even + o * odd
                r16[me, pl.ds(t * RUN, RUN), there] = mixed(lambda c: c, RUN)
                r8[me % 4, pl.ds(t * RUN, RUN), there] = mixed(lambda c: c + 1 - 2 * lax.rem(c, 2), RUN)
                r4[me % 2, pl.ds(t * 2 * RUN, 2 * RUN), there] = mixed(lambda c: lax.div(c, 4) * 4 + 2 - lax.div(lax.rem(c, 4), 2) * 2, 2 * RUN)
        return 0

    lax.fori_loop(0, PAIRS, gather, 0)

    pl.semaphore_wait(barrier, chips)

    def copy(buf, slot, send, recv, peer):
        return pltpu.make_async_remote_copy(
            src_ref=buf.at[slot], dst_ref=buf.at[slot], send_sem=send, recv_sem=recv.at[slot],
            device_id={"seq": peer}, device_id_type=MESH,
        )

    turn = chip % 2
    first = [
        copy(r8, me % 4, send8.at[1], recv8, mate),
        copy(r16, me, send16.at[chips], recv16, mate),
        copy(r16, me, send16.at[0], recv16, sibling),
        copy(r8, me % 4, send8.at[0], recv8, sibling),
        copy(r4, me % 2, send4.at[0], recv4, sibling),
    ]
    others = [(mate_chip + (1 - 2 * turn) * step + chips) % chips for step in range(1, chips - 1)]
    for step, other_chip in enumerate(others):
        first.append(copy(r16, me, send16.at[step + 1], recv16, other_chip * 2 + core))
    for c in first:
        c.start()

    loads[2].wait()
    permute(q_ref, qp)

    def bias_rows(place):
        fill = jnp.where(place < length, 0.0, MASK)
        return jnp.broadcast_to(fill, (LANES // 2, fill.shape[1])).astype(BF16)

    wide = iota((1, LANES), 1) < LANES // 2

    def query(q, side):
        mine = sides[side][0]
        return jnp.concatenate([q * mine, jnp.zeros_like(q) + mine], axis=1)

    def with_ones(v):
        return jnp.concatenate([v, jnp.ones_like(v)], axis=1)

    def own_half(acc, side):
        sums, totals = acc[:, :LANES], acc[:, LANES:]
        return jnp.where(wide, totals, sums) if side else jnp.where(wide, sums, totals)

    column = iota((1, SEG0), 1)
    for t in range(segs):
        place = me * shard + t * SEG0 + ((column & (RUN - 1)) << 4) + bitrev(column >> 5)
        bias0[t] = bias_rows(place)

    def near(j):
        here = pair_lanes(j)
        keys = [
            jnp.concatenate([jnp.transpose(kp[t, :, here]), bias0[t], bias0[t]], axis=0)
            for t in range(segs)
        ]
        values = [with_ones(vp[t, :, here]) for t in range(segs)]

        def unit(t):
            far_t = 1 - t

            def start():
                q = [query(qp[t, :, here], side) for side in range(2)]
                own = dot(jnp.concatenate(q, axis=0), keys[t])
                cross = []
                for side in range(2):
                    mid = slice(side * half, side * half + half)
                    cross.append(dot(q[side][mid], keys[far_t][:, mid]))
                return own, cross

            def take(own, cross):
                rows = []
                extra = []
                for side in range(2):
                    h = 2 * j + side
                    for block in range(2):
                        at = (2 * side + block) * half
                        scores = own[at:at + half]
                        if block != side:
                            rows.append(weigh(scores, peak_of(scores)))
                            continue
                        peak = peak_of(scores, cross[side])
                        weights = weigh(scores, peak)
                        left, right = weights[:, :half], weights[:, half:]
                        if side:
                            right = right + right
                        else:
                            left = left + left
                        rows.append(jnp.concatenate([left, right], axis=1))
                        mid = slice(side * half, side * half + half)
                        extra.append(dot(weigh(cross[side], peak), values[far_t][mid]))
                        peak_s[h, t] = jnp.broadcast_to(peak, (half, LANES))
                acc = dot(jnp.concatenate(rows, axis=0), values[t])
                for side in range(2):
                    for block in range(2):
                        at = (2 * side + block) * half
                        part = acc[at:at + half]
                        if block == side:
                            part = part + extra[side]
                        acc_s[2 * j + side, t, pl.ds(block * half, half), :] = own_half(part, side)

            return start, take

        return [unit(t) for t in range(segs)]

    def near_step(step, _):
        staged(near(2 * step) + near(2 * step + 1))
        return 0

    lax.fori_loop(0, PAIRS // 2, near_step, 0)

    copy(r16, sibling, send16.at[0], recv16, sibling).wait_recv()
    copy(r8, sibling % 4, send8.at[0], recv8, sibling).wait_recv()
    copy(r4, sibling % 2, send4.at[0], recv4, sibling).wait_recv()
    def far(strides, j):
        here = pair_lanes(j)
        there = pair_lanes(j, WIDTH)

        def piece(buf, start, count, shift, keep, owner):
            size = buf.shape[1]
            bits = size.bit_length() - 1
            r = iota((1, count * size), 1)
            place = (
                (owner + (r >> bits)) * shard + ((r >> (bits - 1)) & 1) * SEG0
                + ((r & (RUN - 1)) << 4)
            )
            if size > segs * RUN:
                place = place + ((r >> 5) & 1) * 8
            k = buf[pl.ds(start, count), :, here].reshape(-1, LANES)
            v = buf[pl.ds(start, count), :, there].reshape(-1, LANES)
            return k, v, place, shift, keep

        def listed(pieces):
            k = jnp.concatenate([p[0] for p in pieces], axis=0)
            v = jnp.concatenate([p[1] for p in pieces], axis=0)
            return jnp.transpose(k), v, [p[2:] for p in pieces]

        two, four = me // 2 * 2, me // 4 * 4
        lists = []
        if 4 in strides:
            lists.append((4, listed((
                piece(r16, two, 2, 0, 16, two),
                piece(r8, two % 4, 2, 8, 16, two),
                piece(r4, 0, 2, 4, 8, two),
            ))))
        if 8 in strides:
            lists.append((8, listed((
                piece(r16, four, 4, 0, 16, four), piece(r8, 0, 4, 8, 16, four),
            ))))
        if 16 in strides:
            lists.append((16, listed((piece(r16, 0, n, 0, 16, 0),))))
        def unit(stride, kt, v, places):
            size = SEG0 // stride
            group = CLASSES // stride
            count = segs * size
            starts = [lax.div(home(j, side), group) * size for side in range(2)]

            def start():
                fills = [
                    jnp.concatenate(
                        [
                            bias_rows(place + ((2 * j + side + shift) & (keep - 1)))
                            for place, shift, keep in places
                        ],
                        axis=1,
                    )
                    for side in range(2)
                ]
                q = [
                    query(qp[t, rows_at(starts[side], size), here], side)
                    for side in range(2) for t in range(segs)
                ]
                return (dot(jnp.concatenate(q, axis=0), jnp.concatenate([kt] + fills, axis=0)),)

            def take(scores):
                peak = peak_of(scores)
                acc = dot(weigh(scores, peak), with_ones(v))
                for side in range(2):
                    h = 2 * j + side
                    rows = rows_at(starts[side], size)
                    inner = rows_at(starts[side] - side * half, size)
                    for t in range(segs):
                        at = side * count + t * size
                        acc_t, peak_t = merge(
                            acc_s[h, t, rows, :], peak_s[h, t, inner, :],
                            own_half(acc[at:at + size], side), peak[at:at + size],
                        )
                        acc_s[h, t, rows, :] = acc_t
                        peak_s[h, t, inner, :] = peak_t

            return start, take

        return [unit(stride, *rest) for stride, rest in lists]

    def finish(j):
        here = pair_lanes(j)
        for t in range(segs):
            acc_e, acc_o = acc_s[2 * j, t], acc_s[2 * j + 1, t]
            total = pltpu.roll(jnp.where(wide, acc_o, acc_e), 64, 1)
            done = (jnp.where(wide, acc_e, acc_o) / total).astype(BF16)
            for u in range(2):
                for i in range(CLASSES):
                    at = i * RUN + u * sub
                    out_ref[pl.ds(t * SEG0 + u * half + i * sub, sub), here] = done[at:at + sub]

    def far_step(strides, step, _):
        staged(far(strides, 2 * step) + far(strides, 2 * step + 1))
        if 16 in strides:
            finish(2 * step)
            finish(2 * step + 1)
        return 0

    lax.fori_loop(0, PAIRS // 2, functools.partial(far_step, (4,)), 0)

    def forward(buf, slot, arrived, sent, recv):
        copy(buf, slot, arrived, recv, sibling).wait_recv()
        c = copy(buf, slot, sent, recv, sibling)
        c.start()
        return c

    second = [
        forward(r8, mate % 4, send8.at[1], fwd8.at[0], recv8),
        forward(r16, mate, send16.at[chips], fwd16.at[0], recv16),
    ]
    for step, other_chip in enumerate(others):
        second.append(
            forward(r16, other_chip * 2 + core, send16.at[step + 1], fwd16.at[step + 1], recv16)
        )

    far_mate = mate_chip * 2 + 1 - core
    copy(r8, far_mate % 4, fwd8.at[0], recv8, sibling).wait_recv()
    copy(r16, far_mate, fwd16.at[0], recv16, sibling).wait_recv()
    lax.fori_loop(0, PAIRS // 2, functools.partial(far_step, (8,)), 0)

    for step, other_chip in enumerate(others):
        source = other_chip * 2 + 1 - core
        copy(r16, source, fwd16.at[step + 1], recv16, sibling).wait_recv()
    lax.fori_loop(0, PAIRS // 2, functools.partial(far_step, (16,)), 0)

    for c in first + second:
        c.wait_send()


def restore(len_ref, rows_ref, out_ref):
    half, width = out_ref.shape
    sub = half // CLASSES
    new = iota((half, half), 0)
    old = iota((half, half), 1)
    back = jnp.where(new == ((old & (sub - 1)) << 4) + bitrev(old >> 4), 1.0, 0.0).astype(BF16)
    first = (lax.axis_index("seq") * pl.num_programs(0) + pl.program_id(0)) * half
    valid = first + iota((half, 1), 0) < len_ref[0]
    rows = rows_ref[pl.ds(pl.multiple_of(pl.program_id(0) * half, half), half), :]
    moved = dot(back, rows)
    out_ref[...] = jnp.where(valid, moved, 0.0).astype(BF16)


def per_device(n, query_tiles, key_tiles, value_tiles, slide_length):
    shard = query_tiles.shape[0]
    segs = shard // SEG0
    chips = n // 2
    small = segs * RUN
    vmem = pl.BlockSpec(memory_space=pltpu.VMEM)
    dma = pltpu.SemaphoreType.DMA
    shuffled = pl.pallas_call(
        functools.partial(kernel, n),
        out_shape=pltpu.VMEM((shard, WIDTH), BF16),
        in_specs=[pl.BlockSpec(memory_space=pltpu.SMEM)] + [pl.BlockSpec(memory_space=pl.ANY)] * 3,
        out_specs=vmem,
        scratch_shapes=[
            pltpu.VMEM((shard, WIDTH), BF16),
            pltpu.VMEM((shard, WIDTH), BF16),
            pltpu.VMEM((shard, WIDTH), BF16),
            dma((3,)),
            pltpu.VMEM((segs, SEG0, WIDTH), BF16),
            pltpu.VMEM((segs, SEG0, WIDTH), BF16),
            pltpu.VMEM((segs, SEG0, WIDTH), BF16),
            pltpu.VMEM((n, small, 2 * WIDTH), BF16),
            pltpu.VMEM((4, small, 2 * WIDTH), BF16),
            pltpu.VMEM((2, 2 * small, 2 * WIDTH), BF16),
            pltpu.VMEM((segs, LANES // 2, SEG0), BF16),
            pltpu.VMEM((HEADS, segs, SEG0, LANES), F32),
            pltpu.VMEM((HEADS, segs, SEG0 // 2, LANES), F32),
            dma((chips + 1,)), dma((n,)), dma((2,)), dma((4,)), dma((1,)), dma((2,)),
            dma((chips,)), dma((1,)),
        ],
        compiler_params=pltpu.CompilerParams(
            collective_id=0, has_side_effects=True, vmem_limit_bytes=52 * 1024 * 1024
        ),
        cost_estimate=pl.CostEstimate(
            flops=256 * shard * HEADS * 1024, bytes_accessed=8 * shard * WIDTH,
            transcendentals=shard * HEADS * 1024,
        ),
    )(slide_length, query_tiles, key_tiles, value_tiles)
    block = pl.BlockSpec((SEG0 // 2, WIDTH), lambda i: (i, 0))
    return pl.pallas_call(
        restore,
        grid=(shard // (SEG0 // 2),),
        out_shape=jax.ShapeDtypeStruct((shard, WIDTH), BF16),
        in_specs=[pl.BlockSpec(memory_space=pltpu.SMEM), vmem],
        out_specs=block,
        compiler_params=pltpu.CompilerParams(vmem_limit_bytes=16 * 1024 * 1024),
    )(slide_length, pltpu.with_memory_space_constraint(shuffled, pltpu.VMEM))


def solution(mesh):
    placed = P(("slide", "seq"), None)
    return jax.shard_map(
        functools.partial(per_device, mesh.shape["seq"]),
        mesh=mesh,
        in_specs=(placed, placed, placed, P("slide")),
        out_specs=placed,
        check_vma=False,
    )
```
